32 devices in a mesh: group: 4 (over y, x), shard: 8 (over z, core).
Axes of the slice: x: 2, y: 2, z: 4, core: 2. Of those that a mesh axis runs over, the one named last changes fastest.
Arguments:
- entity_rows: float32 [32768, 200], P(('group', 'shard')), may hold values from -4 to 4
- entity_state: float32 [32768], P(('group', 'shard')), may hold values from 0.5 to 4
- relation_rows: float32 [1387, 200], replicated, may hold values from -6 to 6
- relation_state: float32 [1387], replicated, may hold values from 16 to 160
- conv_weight: bfloat16 [32, 3, 3], replicated, may hold values from -2 to 2
- conv_bias: float32 [32], replicated, may hold values from -3 to 3
- fc_weight: bfloat16 [10368, 200], replicated, may hold values from -0.0625 to 0.0625
- fc_bias: float32 [200], replicated, may hold values from -3 to 3
- head_ids: int32 [2, 4096], P(None, ('group', 'shard')), may hold values from 0 to 1023
- rel_ids: int32 [2, 4096], P(None, ('group', 'shard')), may hold values from 0 to 1386
- tail_ids: int32 [2, 4096], P(None, ('group', 'shard')), may hold values from 0 to 1023
- neg_ids: int32 [2, 1024], P(None, ('group', 'shard')), may hold values from 0 to 1023
Outputs:
- new_entity_rows: float32 [32768, 200], P(('group', 'shard'))
- new_entity_state: float32 [32768], P(('group', 'shard'))
- new_relation_rows: float32 [1387, 200], replicated
- new_relation_state: float32 [1387], replicated
The draws below stay inside these ranges and needn't reach their ends.
All inputs are finite; a program needn't handle non-finite values.
Results may differ from the reference program's by a relative error of at most 0.002.
Values may be sent and summed in bfloat16 or wider, within the bound.
No kernel may reach another device: no remote copies, remote signals or barrier semaphores. Data moves between devices by JAX's collectives and lax.ppermute only.
A program may use at most 128 MiB of HBM per device.

```python
import math
import jax
import jax.numpy as jnp
import numpy as np
from jax import lax

EMB_H = 10
EMB_W = 20
D = 200
FILTERS = 32
FLAT = 10368
REL = 1387
ENT_DEV = 1024
TRI_DEV = 128
NEG_DEV = 32
ROUNDS = 2
NEG_SPAN = 256
ENTITIES = 32768
TRI_ALL = 4096
NEG_ALL = 1024
N_GROUP = 4
N_SHARD = 8


def set_ends(array, rng, least, top_value):
    spot = [jax.random.randint(jax.random.fold_in(rng, axis), (), 0, length) for axis, length in enumerate(array.shape)]
    longest = array.shape.index(max(array.shape))
    next_to = spot[:longest] + [(spot[longest] + 1) % array.shape[longest]] + spot[longest + 1:]
    return array.at[tuple(spot)].set(least).at[tuple(next_to)].set(top_value)


def block_levels(stream_key, shape, cuts, least, top_value):
    gain = 1.0
    for position, parts in cuts:
        draws = jax.random.uniform(jax.random.fold_in(jax.random.fold_in(stream_key, 6), position), (parts,), jnp.float32, least / len(cuts), top_value / len(cuts))
        gain = gain * jnp.repeat(jnp.exp(draws), shape[position] // parts).reshape((-1,) + (1,) * (len(shape) - 1 - position))
    return gain


def rank_table(number_of, skew):
    weights = [(1 << 20) // math.isqrt(standing ** skew) + 1 for standing in range(1, number_of + 1)]
    scale = 1 + sum(weights) // (1 << 30)
    return np.cumsum(np.array([max(1, weight // scale) for weight in weights]))


def ranked_ids(key, extent, count, lean):
    listing = rank_table(count, lean)
    pick = jax.random.randint(jax.random.fold_in(key, 1), extent, 0, int(listing[count - 1]))
    rank = jnp.searchsorted(jnp.asarray(listing, jnp.int32), pick, side="right")
    return jax.random.permutation(jax.random.fold_in(key, 2), count)[rank].astype(jnp.int32)


def normal_values(stream_key, extent, deviation, most, cuts=(), kind=jnp.bfloat16):
    factor_of = block_levels(stream_key, extent, cuts, -0.22, 0.18) if cuts else 1.0
    drawn = jax.random.normal(stream_key, extent, jnp.float32) * deviation * factor_of
    return jnp.minimum(jnp.maximum(drawn, -most), most).astype(kind)


def setup_inputs(seed: int = 0) -> dict:
    key_list = jax.random.split(jax.random.key(seed), 13)
    return {
        "entity_rows": normal_values(key_list[0], (ENTITIES, D), 0.3, 4.0, ((0, 32),), jnp.float32),
        "entity_state": jnp.clip(jnp.exp(math.log(4.0) - 2.0794415 * jax.random.uniform(key_list[1], (ENTITIES,), jnp.float32) ** block_levels(key_list[1], (ENTITIES,), ((0, 32),), -0.2, 0.2)), 0.5, 4.0),
        "relation_rows": normal_values(key_list[2], (REL, D), 0.5, 6.0, (), jnp.float32),
        "relation_state": jnp.clip(jnp.exp(jax.random.uniform(key_list[3], (REL,), jnp.float32, math.log(16.0), math.log(160.0))), 16.0, 160.0),
        "conv_weight": normal_values(key_list[4], (FILTERS, 3, 3), 9 ** -0.5, 2.0),
        "conv_bias": normal_values(key_list[5], (FILTERS,), 0.3, 3.0, (), jnp.float32),
        "fc_weight": normal_values(key_list[6], (FLAT, D), FLAT ** -0.5, 0.0625),
        "fc_bias": normal_values(key_list[7], (D,), 0.3, 3.0, (), jnp.float32),
        "head_ids": set_ends(ranked_ids(key_list[8], (ROUNDS, TRI_ALL), ENT_DEV, 2), jax.random.fold_in(key_list[8], 3), 0, ENT_DEV - 1).astype(jnp.int32),
        "rel_ids": set_ends(ranked_ids(key_list[9], (ROUNDS, TRI_ALL), REL, 2), jax.random.fold_in(key_list[9], 3), 0, REL - 1).astype(jnp.int32),
        "tail_ids": set_ends(jax.random.randint(key_list[10], (ROUNDS, TRI_ALL), 0, ENT_DEV), jax.random.fold_in(key_list[10], 1), 0, ENT_DEV - 1).astype(jnp.int32),
        "neg_ids": set_ends(jax.random.randint(key_list[11], (ROUNDS, NEG_ALL), 0, ENT_DEV), jax.random.fold_in(key_list[11], 1), 0, ENT_DEV - 1).astype(jnp.int32),
    }


negative_weight = 0.03125
learn_rate = 0.5

def silu_slope(values):
    sigma = jax.nn.sigmoid(values)
    return sigma * (1.0 + values * (1.0 - sigma))

def conv_forward(picture, conv_weight, conv_bias):
    height = picture.shape[0] - 2
    across = picture.shape[1] - 2
    patches = jnp.stack([picture[row_off:row_off + height, col_off:col_off + across] for row_off in range(3) for col_off in range(3)])
    filters = conv_weight.reshape(FILTERS, 9).astype(jnp.float32)
    result = jnp.einsum('fk,kijt->fijt', filters, patches.astype(jnp.float32))
    return result + conv_bias[:, None, None, None]

def conv_backward(pre1_grad, conv_weight):
    filters = conv_weight.reshape(FILTERS, 9).astype(jnp.float32)
    spread = jnp.einsum('fk,fijt->kijt', filters, pre1_grad.astype(jnp.float32))
    height = spread.shape[1]
    across = spread.shape[2]
    total = jnp.zeros((height + 2, across + 2, spread.shape[3]), jnp.float32)
    for offset in range(9):
        row_off, col_off = divmod(offset, 3)
        total = total.at[row_off:row_off + height, col_off:col_off + across].add(spread[offset])
    return total

def block_pass(head_rows, rel_rows, tail_rows, negset, conv_weight, conv_bias, fc_weight, fc_bias):
    number = head_rows.shape[0]
    picture = jnp.concatenate([head_rows.reshape(number, EMB_H, EMB_W), rel_rows.reshape(number, EMB_H, EMB_W)], axis=1)
    picture = jnp.transpose(picture, (1, 2, 0))
    pre1 = conv_forward(picture, conv_weight, conv_bias)
    act = jax.nn.silu(pre1).astype(jnp.bfloat16).reshape(FLAT, number)
    pre2 = jnp.dot(fc_weight.T, act, preferred_element_type=jnp.float32) + fc_bias[:, None]
    query = jax.nn.silu(pre2).astype(jnp.bfloat16)
    tail_cols = tail_rows.T.astype(jnp.float32)
    pos_score = lax.optimization_barrier(jnp.sum(query.astype(jnp.float32) * tail_cols, axis=0))
    neg_score = jnp.dot(negset, query, preferred_element_type=jnp.float32)
    pos_grad = -jax.nn.sigmoid(-pos_score)
    neg_grad = (negative_weight * jax.nn.sigmoid(neg_score)).astype(jnp.bfloat16)
    query_grad = pos_grad[None, :] * tail_cols + lax.dot_general(negset, neg_grad, (((0,), (0,)), ((), ())), preferred_element_type=jnp.float32)
    pre2_grad = (query_grad * silu_slope(pre2)).astype(jnp.bfloat16)
    act_grad = jnp.dot(fc_weight, pre2_grad, preferred_element_type=jnp.float32)
    pre1_grad = (act_grad.reshape(pre1.shape) * silu_slope(pre1)).astype(jnp.bfloat16)
    picture_grad = conv_backward(pre1_grad, conv_weight)
    head_grad = jnp.transpose(picture_grad[:EMB_H], (2, 0, 1)).reshape(number, D)
    relation_grad = jnp.transpose(picture_grad[EMB_H:], (2, 0, 1)).reshape(number, D)
    tail_grad = (pos_grad[None, :] * query.astype(jnp.float32)).T
    negset_grad = lax.dot_general(neg_grad, query, (((1,), (1,)), ((), ())), preferred_element_type=jnp.float32)
    return (head_grad, relation_grad, tail_grad, negset_grad)

def adagrad(rows, state, gradient):
    state = state + lax.optimization_barrier(jnp.mean(gradient * gradient, axis=1))
    rows = rows - learn_rate * gradient / jnp.sqrt(state)[:, None]
    return (rows, state)

def reference(entity_rows, entity_state, relation_rows, relation_state, conv_weight, conv_bias, fc_weight, fc_bias, head_ids, rel_ids, tail_ids, neg_ids):
    blocks = N_GROUP * N_SHARD
    pick_rows = jax.vmap(jax.vmap(lambda table_rows, row_index: table_rows[row_index]))
    for round_index in range(ROUNDS):
        partner_bit = 1 << round_index
        partner_group = np.arange(N_GROUP) ^ partner_bit
        ent_bf = entity_rows.astype(jnp.bfloat16).reshape(N_GROUP, N_SHARD, ENT_DEV, D)
        rel_bf = relation_rows.astype(jnp.bfloat16)
        partner = ent_bf[partner_group]
        heads = head_ids[round_index].reshape(N_GROUP, N_SHARD, TRI_DEV)
        tails = tail_ids[round_index].reshape(N_GROUP, N_SHARD, TRI_DEV)
        negatives = neg_ids[round_index].reshape(N_GROUP, N_SHARD, NEG_DEV)
        head_rows = pick_rows(ent_bf, heads).reshape(blocks, TRI_DEV, D)
        tail_rows = pick_rows(partner, tails).reshape(blocks, TRI_DEV, D)
        rel_rows = rel_bf[rel_ids[round_index]].reshape(blocks, TRI_DEV, D)
        negset = pick_rows(partner, negatives).reshape(N_GROUP, NEG_SPAN, D)
        negset_each = jnp.repeat(negset, N_SHARD, axis=0)

        def per_block(inputs):
            return block_pass(inputs[0], inputs[1], inputs[2], inputs[3], conv_weight, conv_bias, fc_weight, fc_bias)
        head_grad, relation_grad, tail_grad, negset_grad = lax.map(per_block, (head_rows, rel_rows, tail_rows, negset_each))
        negset_sum = negset_grad.reshape(N_GROUP, N_SHARD, NEG_SPAN, D).sum(axis=1).reshape(N_GROUP * N_SHARD * NEG_DEV, D)
        own_base = (jnp.arange(blocks, dtype=jnp.int32) * ENT_DEV).reshape(N_GROUP, N_SHARD, 1)
        partner_base = ((jnp.asarray(partner_group, dtype=jnp.int32)[:, None] * N_SHARD + jnp.arange(N_SHARD, dtype=jnp.int32)[None, :]) * ENT_DEV)[:, :, None]
        head_index = (own_base + heads).reshape(-1)
        tail_index = (partner_base + tails).reshape(-1)
        neg_index = (partner_base + negatives).reshape(-1)
        entity_grad = jnp.zeros((ENTITIES, D), jnp.float32)
        entity_grad = entity_grad.at[head_index].add(head_grad.reshape(-1, D))
        entity_grad = entity_grad.at[tail_index].add(tail_grad.reshape(-1, D))
        entity_grad = entity_grad.at[neg_index].add(negset_sum)
        rel_total = jnp.zeros((REL, D), jnp.float32).at[rel_ids[round_index]].add(relation_grad.reshape(-1, D))
        entity_rows, entity_state = adagrad(entity_rows, entity_state, entity_grad)
        relation_rows, relation_state = adagrad(relation_rows, relation_state, rel_total)
    return (entity_rows, entity_state, relation_rows, relation_state)
```

```python
import functools

import jax
import jax.numpy as jnp
from jax import lax
from jax.experimental import pallas as pl
from jax.experimental.pallas import tpu as pltpu
from jax.sharding import PartitionSpec as P

EMB_W = 20
D = 200
FILTERS = 32
PIXELS = 400
SIDE = 18
PAIRS = 9
WINDOW = 80
WIDE = 1152
PACK = 208
LANES = 128
ROUNDS = 2
SPLITS = ((0, 256), (256, 512), (512, 768), (768, 1024), (1024, 1152))

negative_weight = 0.03125
learn_rate = 0.5

f32 = jnp.float32
bf16 = jnp.bfloat16
BOTH = ("group", "shard")
PARAMS = pltpu.CompilerParams(vmem_limit_bytes=48 * 1024 * 1024)
VMEM = pl.BlockSpec(memory_space=pltpu.VMEM)
SMEM = pl.BlockSpec(memory_space=pltpu.SMEM)


def sigmoid(values):
    return 0.5 * jnp.tanh(0.5 * values) + 0.5


def rows_nt(left, right):
    return lax.dot_general(left, right, (((1,), (1,)), ((), ())), preferred_element_type=f32)


def rows_tn(left, right):
    return lax.dot_general(left, right, (((0,), (0,)), ((), ())), preferred_element_type=f32)


def as_columns(row):
    return jnp.transpose(jnp.broadcast_to(row.astype(f32), (LANES, LANES)))


def one_hot_rows(ids_row, count):
    wide = as_columns(ids_row)
    lane = lax.broadcasted_iota(jnp.int32, (LANES, LANES), 1)
    parts = [
        jnp.where(wide == (lane + first).astype(f32), 1.0, 0.0).astype(bf16)
        for first in range(0, count, LANES)
    ]
    return jnp.concatenate(parts, axis=1)


def halves(values):
    high = values.astype(bf16)
    return high, (values - high.astype(f32)).astype(bf16)


def prepare_kernel(fc_ref, taps_ref, fc_out, band_out, band_t_out, left, right):
    rows = fc_ref.shape[0]
    step = rows // 16

    def widen(index, carry):
        at = pl.ds(pl.multiple_of(index * step, 8), step)
        block = fc_ref[at, :].astype(f32)
        left[at, :] = block[:, :LANES]
        right[at, : D - LANES] = block[:, LANES:]
        return carry

    lax.fori_loop(0, 16, widen, 0)
    spots = SIDE * SIDE

    def regroup(index, carry):
        low = left[pl.ds(index, FILTERS, stride=spots), :]
        high = right[pl.ds(index, FILTERS, stride=spots), :]
        at = pl.ds(pl.multiple_of(index * FILTERS, FILTERS), FILTERS)
        fc_out[at, :LANES] = low.astype(bf16)
        fc_out[at, LANES:] = high[:, : D - LANES].astype(bf16)
        return carry

    lax.fori_loop(0, spots, regroup, 0, unroll=4)
    group = lax.broadcasted_iota(jnp.int32, (WINDOW, WIDE), 1) >> 5
    lower = jnp.where(group >= SIDE, 1, 0)
    start = group + (EMB_W - SIDE) * lower
    gap = lax.broadcasted_iota(jnp.int32, (WINDOW, WIDE), 0) - start
    band = jnp.zeros((WINDOW, WIDE), f32)
    for row_off in range(3):
        for col_off in range(3):
            tap = row_off * 3 + col_off
            hit = gap == EMB_W * row_off + col_off
            band = jnp.where(hit, taps_ref[tap : tap + 1, :], band)
    band_out[...] = band.astype(bf16)
    band_t_out[...] = jnp.transpose(
        jnp.concatenate([band, jnp.zeros((LANES - WINDOW, WIDE), f32)], axis=0)
    ).astype(bf16)


def prepare(fc_weight, taps):
    rows = fc_weight.shape[0]
    return pl.pallas_call(
        prepare_kernel,
        out_shape=(
            jax.ShapeDtypeStruct((rows, D), bf16),
            jax.ShapeDtypeStruct((WINDOW, WIDE), bf16),
            jax.ShapeDtypeStruct((WIDE, LANES), bf16),
        ),
        in_specs=[VMEM] * 2,
        out_specs=[VMEM] * 3,
        scratch_shapes=[pltpu.VMEM((rows, LANES), f32), pltpu.VMEM((rows, LANES), f32)],
        compiler_params=PARAMS,
        name="prepare",
    )(fc_weight, taps)


def pass_kernel(
    ids_ref, ent_ref, rel_ref, tail_ref, neg_ref, band_ref, band_t_ref, bias_ref, fc_ref, fcb_ref,
    pack_out, head_out, tail_out, neg_out,
    picture, slopes, total,
):
    heads = ids_ref[0:1, :]
    relations = ids_ref[1:2, :]
    ent_bf = ent_ref[...].astype(bf16)
    rel_bf = rel_ref[...].astype(bf16)
    head_rows = jnp.dot(one_hot_rows(heads, ent_bf.shape[0]), ent_bf, preferred_element_type=f32)
    rel_rows = jnp.dot(one_hot_rows(relations, rel_bf.shape[0]), rel_bf, preferred_element_type=f32)
    picture[:D, :] = jnp.transpose(head_rows)
    picture[D:, :] = jnp.transpose(rel_rows)
    number = LANES

    def forward(pair, pre2):
        at = pl.ds(pl.multiple_of(pair * 2 * EMB_W, 8), WINDOW)
        window = jnp.transpose(picture[at, :]).astype(bf16)
        for first, last in SPLITS:
            pre1 = (
                jnp.dot(window, band_ref[:, first:last], preferred_element_type=f32)
                + bias_ref[:, first:last]
            )
            sigma = sigmoid(pre1)
            act = pre1 * sigma
            slopes[pair, :, first:last] = sigma + act * (1.0 - sigma)
            pre2 = pre2 + jnp.dot(
                act.astype(bf16), fc_ref[pair, first:last, :], preferred_element_type=f32
            )
        return pre2

    pre2 = lax.fori_loop(0, PAIRS, forward, jnp.zeros((number, D), f32)) + fcb_ref[...]
    sigma = sigmoid(pre2)
    value = pre2 * sigma
    slope2 = sigma + value * (1.0 - sigma)
    query = value.astype(bf16)
    query32 = query.astype(f32)
    tails = tail_ref[...].astype(f32)
    pos_score = jnp.sum(query32 * tails, axis=1, keepdims=True)
    pos_grad = -sigmoid(-pos_score)
    negset = neg_ref[...]
    neg_grad = (negative_weight * sigmoid(rows_nt(query, negset))).astype(bf16)
    query_grad = pos_grad * tails + jnp.dot(neg_grad, negset, preferred_element_type=f32)
    pre2_grad = (query_grad * slope2).astype(bf16)
    tail_out[...] = pos_grad * query32
    neg_out[...] = rows_tn(neg_grad, query)
    total[...] = jnp.zeros_like(total)

    def backward(pair, carry):
        part = jnp.zeros((number, LANES), f32)
        for first, last in SPLITS:
            act_grad = rows_nt(pre2_grad, fc_ref[pair, first:last, :])
            pre1_grad = (act_grad * slopes[pair, :, first:last]).astype(bf16)
            part = part + jnp.dot(
                pre1_grad, band_t_ref[first:last, :], preferred_element_type=f32
            )
        at = pl.ds(pl.multiple_of(pair * 2 * EMB_W, 8), WINDOW)
        total[at, :] = total[at, :] + jnp.transpose(part)[:WINDOW, :]
        return carry

    lax.fori_loop(0, PAIRS, backward, 0)
    head_out[...] = total[:D, :]
    high = relations >> 6
    low = relations - (high << 6)
    spare = lax.broadcasted_iota(jnp.int32, (PACK - D, number), 0)
    codes = jnp.where(spare == 0, high, jnp.where(spare == 1, low, 0)).astype(f32)
    pack_out[...] = jnp.concatenate([total[D:, :], codes], axis=0).astype(bf16)


def local_pass(ids, ent, rel, tails, negset, band, band_t, bias, fc, fc_bias):
    number = tails.shape[0]
    return pl.pallas_call(
        pass_kernel,
        out_shape=(
            jax.ShapeDtypeStruct((PACK, number), bf16),
            jax.ShapeDtypeStruct((D, number), f32),
            jax.ShapeDtypeStruct((number, D), f32),
            jax.ShapeDtypeStruct((negset.shape[0], D), f32),
        ),
        in_specs=[VMEM] * 10,
        out_specs=[VMEM] * 4,
        scratch_shapes=[
            pltpu.VMEM((PIXELS, number), f32),
            pltpu.VMEM((PAIRS, number, WIDE), f32),
            pltpu.VMEM((PIXELS, number), f32),
        ],
        compiler_params=PARAMS,
        name="local_pass",
    )(ids, ent, rel, tails, negset, band, band_t, bias, fc, fc_bias)


def step_rows(rows, state_row, gradient):
    state = as_columns(state_row)
    state = state + jnp.mean(gradient * gradient, axis=1, keepdims=True)
    scale = learn_rate * lax.rsqrt(state)
    rows = rows - gradient * scale[:, :1]
    return rows, jnp.transpose(state)[:1, :]


def entity_kernel(
    more, ids_ref, rows_ref, state_ref, head_ref, tail_ref, neg_ref, *outs
):
    rows_out, state_out = outs[:2]
    count = rows_ref.shape[0]
    number = tail_ref.shape[0]
    negatives = neg_ref.shape[0]
    grads = jnp.concatenate([jnp.transpose(head_ref[...]), tail_ref[...], neg_ref[...]], axis=0)
    high, low = halves(grads)
    named = jnp.concatenate(
        [ids_ref[0:1, :], ids_ref[2:3, :], ids_ref[3:4, :negatives]], axis=1
    )
    for block in range(count // LANES):
        at = slice(block * LANES, (block + 1) * LANES)
        place = lax.broadcasted_iota(jnp.int32, (LANES, named.shape[1]), 0) + block * LANES
        hit = jnp.where(place == named, 1.0, 0.0).astype(bf16)
        gradient = jnp.dot(hit, high, preferred_element_type=f32) + jnp.dot(
            hit, low, preferred_element_type=f32
        )
        new_rows, new_state = step_rows(rows_ref[at, :], state_ref[block : block + 1, :], gradient)
        rows_out[at, :] = new_rows
        state_out[block : block + 1, :] = new_state
    if more:
        table = rows_out[...].astype(bf16)
        for index, size in ((4, number), (5, negatives)):
            picked = jnp.dot(
                one_hot_rows(ids_ref[index : index + 1, :], count), table, preferred_element_type=f32
            )
            outs[2][(index - 4) * number : (index - 4) * number + size, :] = picked[:size].astype(bf16)


def entity_update(more, ids, rows, state, head_grad, tail_grad, neg_grad):
    out_shape = [
        jax.ShapeDtypeStruct(rows.shape, f32),
        jax.ShapeDtypeStruct(state.shape, f32),
    ]
    if more:
        out_shape.append(
            jax.ShapeDtypeStruct((tail_grad.shape[0] + neg_grad.shape[0], D), bf16)
        )
    return pl.pallas_call(
        functools.partial(entity_kernel, more),
        out_shape=out_shape,
        in_specs=[VMEM] * 6,
        out_specs=[VMEM] * len(out_shape),
        compiler_params=PARAMS,
        name="entity_update",
    )(ids, rows, state, head_grad, tail_grad, neg_grad)


def relation_kernel(place_ref, packs_ref, rows_ref, state_ref, rows_out, state_out, grads, names):
    sources = packs_ref.shape[0]

    def lay(index, carry):
        for part in range(2):
            block = packs_ref[place_ref[2 * index + part]]
            grads[index, :, part * LANES : (part + 1) * LANES] = block
            codes = block[PACK - 16 :, :].astype(f32)
            names[index, :, part * LANES : (part + 1) * LANES] = (
                codes[8:9, :] * 64.0 + codes[9:10, :]
            ).astype(jnp.int32)
        return carry

    lax.fori_loop(0, sources // 2, lay, 0)

    def block_step(first, size):
        place = lax.broadcasted_iota(jnp.int32, (size, 2 * LANES), 0) + first

        def add(index, acc):
            hit = jnp.where(place == names[index], 1.0, 0.0).astype(bf16)
            return acc + rows_nt(hit, grads[index])

        return lax.fori_loop(0, sources // 2, add, jnp.zeros((size, PACK), f32), unroll=8)

    count = rows_out.shape[0]
    for block in range(rows_ref.shape[0] // LANES):
        first = block * LANES
        gradient = block_step(first, LANES)[:, :D]
        new_rows, new_state = step_rows(
            rows_ref[first : first + LANES, :], state_ref[block : block + 1, :], gradient
        )
        size = min(LANES, count - first)
        rows_out[first : first + size, :] = new_rows[:size, :]
        state_out[block : block + 1, :] = new_state


def relation_update(place, packs, rows, state, out_rows):
    sources = packs.shape[0]
    return pl.pallas_call(
        relation_kernel,
        out_shape=(
            jax.ShapeDtypeStruct((out_rows, D), f32),
            jax.ShapeDtypeStruct(state.shape, f32),
        ),
        in_specs=[SMEM] + [VMEM] * 3,
        out_specs=[VMEM] * 2,
        scratch_shapes=[
            pltpu.VMEM((sources // 2, PACK, 2 * LANES), bf16),
            pltpu.VMEM((sources // 2, 1, 2 * LANES), jnp.int32),
        ],
        compiler_params=PARAMS,
        name="relation_update",
    )(place, packs, rows, state)


def swapped(bits):
    out = list(bits)
    for index in range(0, len(out) - 1, 2):
        out[index], out[index + 1] = out[index + 1], out[index]
    return out


class Plan:
    def __init__(self, groups, shards):
        self.total = groups * shards
        self.shards = shards
        near = [1 << bit for bit in range(1, shards.bit_length() - 1)]
        far = [shards << bit for bit in range(groups.bit_length() - 1)]
        self.even = near + far
        self.odd = swapped(near) + swapped(far)
        steps = [self.route(a, b) for a, b in zip(self.even, self.odd)]
        core = self.route(1, 1)
        self.within = steps[: len(near)] + [core]
        self.across = steps + [core]

    def route(self, even, odd):
        return [(at, at ^ (odd if at & 1 else even)) for at in range(self.total)]

    def partner(self, bit):
        mask = self.shards << bit
        return self.route(mask, mask)

    def places(self, me):
        source = jnp.arange(self.total, dtype=jnp.int32)
        differ = source ^ me
        even = jnp.zeros_like(source)
        odd = jnp.zeros_like(source)
        for step, (one, other) in enumerate(zip(self.even, self.odd)):
            even = even + jnp.where((differ & one) != 0, 1 << step, 0)
            odd = odd + jnp.where((differ & other) != 0, 1 << step, 0)
        spot = jnp.where((source & 1) == 0, even, odd)
        return spot + jnp.where((differ & 1) != 0, 1 << len(self.even), 0)


def send(block, route):
    return lax.ppermute(block, BOTH, route)


def doubled(block, routes):
    for route in routes:
        block = jnp.concatenate([block, send(block, route)], axis=0)
    return block


def halved(block, routes):
    for route in reversed(routes):
        half = block.shape[0] // 2
        block = block[:half] + send(block[half:], route)
    return block


def shards(
    plan,
    entity_rows,
    entity_state,
    relation_rows,
    relation_state,
    conv_weight,
    conv_bias,
    fc_weight,
    fc_bias,
    head_ids,
    rel_ids,
    tail_ids,
    neg_ids,
):
    number = head_ids.shape[1]
    count = relation_rows.shape[0]
    spare = -count % LANES
    me = lax.axis_index("group") * plan.shards + lax.axis_index("shard")
    wanted = jnp.concatenate([tail_ids, neg_ids], axis=1)
    requested = [send(wanted[r], plan.partner(r)) for r in range(ROUNDS)]
    answer = entity_rows[requested[0]].astype(bf16)

    taps = jnp.tile(conv_weight.reshape(FILTERS, 9).T.astype(f32), (1, WIDE // FILTERS))
    bias = jnp.tile(conv_bias[None, :], (1, WIDE // FILTERS))
    fc, band, band_t = prepare(fc_weight, taps)
    fc = fc.reshape(PAIRS, WIDE, D)
    rel = jnp.pad(relation_rows, ((0, spare), (0, 0)))
    rel_state = jnp.pad(relation_state, (0, spare), constant_values=1.0).reshape(-1, LANES)
    ent = entity_rows
    ent_state = entity_state.reshape(-1, LANES)
    place = plan.places(me)

    def lane_row(ids):
        return jnp.pad(ids, (0, LANES - ids.shape[0]))[None, :]

    for r in range(ROUNDS):
        last = r == ROUNDS - 1
        answered = send(answer, plan.partner(r))
        negset = doubled(answered[number:], plan.within)
        following = requested[min(r + 1, ROUNDS - 1)]
        ids = jnp.concatenate(
            [
                head_ids[r][None, :],
                rel_ids[r][None, :],
                requested[r][None, :number],
                lane_row(requested[r][number:]),
                following[None, :number],
                lane_row(following[number:]),
                jnp.zeros((2, LANES), jnp.int32),
            ],
            axis=0,
        )
        pack, head_grad, tail_grad, neg_part = local_pass(
            ids, ent, rel, answered[:number], negset, band, band_t, bias, fc, fc_bias[None, :]
        )
        share = halved(neg_part, plan.within)
        tail_back = send(tail_grad, plan.partner(r))
        neg_back = send(share, plan.partner(r))
        packs = doubled(pack[None], plan.across)
        outs = entity_update(not last, ids, ent, ent_state, head_grad, tail_back, neg_back)
        ent, ent_state = outs[:2]
        if not last:
            answer = outs[2]
        rel, rel_state = relation_update(
            place, packs, rel, rel_state, count if last else count + spare
        )
    return (ent, ent_state.reshape(-1), rel, rel_state.reshape(-1)[:count])


def solution(mesh):
    plan = Plan(mesh.shape["group"], mesh.shape["shard"])
    in_specs = (
        P(BOTH, None),
        P(BOTH),
        P(),
        P(),
        P(),
        P(),
        P(),
        P(),
        P(None, BOTH),
        P(None, BOTH),
        P(None, BOTH),
        P(None, BOTH),
    )
    out_specs = (P(BOTH, None), P(BOTH), P(), P())
    return jax.shard_map(
        functools.partial(shards, plan),
        mesh=mesh,
        in_specs=in_specs,
        out_specs=out_specs,
        check_vma=False,
    )
```

```python
import functools

import jax
import jax.numpy as jnp
from jax import lax
from jax.experimental import pallas as pl
from jax.experimental.pallas import tpu as pltpu
from jax.sharding import PartitionSpec as P

EMB_W = 20
D = 200
FILTERS = 32
PIXELS = 400
SIDE = 18
PAIRS = 9
WINDOW = 80
WIDE = 1152
PACK = 208
LANES = 128
ROUNDS = 2

negative_weight = 0.03125
learn_rate = 0.5

f32 = jnp.float32
bf16 = jnp.bfloat16
i32 = jnp.int32
BOTH = ("group", "shard")
VMEM = pl.BlockSpec(memory_space=pltpu.VMEM)
SMEM = pl.BlockSpec(memory_space=pltpu.SMEM)


def shaped(shape, dtype=f32):
    return jax.ShapeDtypeStruct(shape, dtype)


def call(kernel, name, micros, out_shape, args, scratch=(), scalars=0, limit=40):
    return pl.pallas_call(
        kernel,
        out_shape=out_shape,
        in_specs=[SMEM] * scalars + [VMEM] * (len(args) - scalars),
        out_specs=[VMEM] * len(out_shape),
        scratch_shapes=list(scratch),
        compiler_params=pltpu.CompilerParams(vmem_limit_bytes=limit * 1024 * 1024),
        cost_estimate=pl.CostEstimate(
            flops=int(micros * 1e9), bytes_accessed=int(micros * 3e6), transcendentals=0
        ),
        name=name,
    )(*args)


def sigmoid(values):
    return 0.5 * jnp.tanh(0.5 * values) + 0.5


def dot(left, right):
    return jnp.dot(left, right, preferred_element_type=f32)


def dot_nt(left, right):
    return lax.dot_general(left, right, (((1,), (1,)), ((), ())), preferred_element_type=f32)


def dot_tn(left, right):
    return lax.dot_general(left, right, (((0,), (0,)), ((), ())), preferred_element_type=f32)


def as_column(row):
    return jnp.transpose(jnp.broadcast_to(row.astype(f32), (LANES, LANES)))


def hits(names_row, count, first=0):
    spot = lax.broadcasted_iota(i32, (count, names_row.shape[1]), 0) + first
    return jnp.where(spot == names_row, 1.0, 0.0).astype(bf16)


def halves(values):
    high = values.astype(bf16)
    return high, (values - high.astype(f32)).astype(bf16)


def padded(values, lanes):
    rest = lanes - values.shape[1]
    return jnp.concatenate([values, jnp.zeros((values.shape[0], rest), values.dtype)], axis=1)


def turned(values):
    rows = values.shape[0]
    if rows < LANES:
        values = jnp.concatenate([values, jnp.zeros((LANES - rows, values.shape[1]), f32)], axis=0)
    return jnp.transpose(values)


def wanted_kernel(tails_ref, negatives_ref, *outs):
    for index, out in enumerate(outs):
        out[0:1, :] = tails_ref[index : index + 1, :]
        out[1:2, :] = padded(negatives_ref[index : index + 1, :], LANES)


def pick_answer(table, ids_ref, negatives, out):
    count = table.shape[1]
    number = out.shape[0] - negatives
    tails = dot(table, hits(ids_ref[0:1, :], count))
    out[:number, :] = jnp.transpose(tails).astype(bf16)
    negs = dot(table, hits(ids_ref[1:2, :], count))
    out[number:, :] = jnp.transpose(negs)[:negatives, :].astype(bf16)


def answer_kernel(negatives, ids_ref, ent_ref, out):
    pick_answer(ent_ref[...].astype(bf16), ids_ref, negatives, out)


def prepare_kernel(fc_ref, taps_ref, fc_out, band_out, band_t_out, left, right):
    blank = jnp.zeros((2 * LANES - D, LANES), f32)
    for index in range(fc_ref.shape[1] // LANES):
        at = slice(index * LANES, (index + 1) * LANES)
        block = fc_ref[:, at].astype(f32)
        left[at, :] = jnp.transpose(block[:LANES])
        right[at, :] = jnp.transpose(jnp.concatenate([block[LANES:], blank], axis=0))
    spots = SIDE * SIDE

    def regroup(index, carry):
        low = left[pl.ds(index, FILTERS, stride=spots), :]
        high = right[pl.ds(index, FILTERS, stride=spots), :]
        at = pl.ds(pl.multiple_of(index * FILTERS, FILTERS), FILTERS)
        fc_out[at, :LANES] = low.astype(bf16)
        fc_out[at, LANES:] = high[:, : D - LANES].astype(bf16)
        return carry

    lax.fori_loop(0, spots, regroup, 0, unroll=9)
    group = lax.broadcasted_iota(i32, (WINDOW, WIDE), 1) >> 5
    start = group + jnp.where(group >= SIDE, EMB_W - SIDE, 0)
    gap = lax.broadcasted_iota(i32, (WINDOW, WIDE), 0) - start
    band = jnp.zeros((WINDOW, WIDE), f32)
    for row_off in range(3):
        for col_off in range(3):
            tap = row_off * 3 + col_off
            hit = gap == EMB_W * row_off + col_off
            band = jnp.where(hit, taps_ref[tap : tap + 1, :], band)
    band_out[...] = band.astype(bf16)
    band_t_out[...] = jnp.transpose(
        jnp.concatenate([band, jnp.zeros((LANES - WINDOW, WIDE), f32)], axis=0)
    ).astype(bf16)


def rows_kernel(ids_ref, rel_ref, state_ref, first_out, later_out, state_out, table):
    count = rel_ref.shape[1]
    whole = count // LANES * LANES
    table[:, :whole] = rel_ref[:, :whole]
    rest = jnp.concatenate(
        [rel_ref[:, whole:], jnp.zeros((D, LANES - count + whole), f32)], axis=1
    )
    table[:, whole:] = rest
    values = table[...]
    wide = values.shape[1]
    high = values.astype(bf16)
    first_out[...] = dot(high, hits(ids_ref[0:1, :], wide))
    left = values - high.astype(f32)
    middle = left.astype(bf16)
    low = (left - middle.astype(f32)).astype(bf16)
    hit = hits(ids_ref[1:2, :], wide)
    later_out[...] = dot(high, hit) + dot(middle, hit) + dot(low, hit)
    sums = padded(state_ref[...], wide)
    column = lax.broadcasted_iota(i32, (wide // LANES, LANES, LANES), 1)
    names = ids_ref[1:2, :]
    total = jnp.zeros((LANES, LANES), f32)
    for block in range(wide // LANES):
        states = as_column(sums[:, block * LANES : (block + 1) * LANES])
        spot = lax.broadcasted_iota(i32, (LANES, LANES), 0) + block * LANES
        total = total + jnp.where(spot == names, states, 0.0)
    state_out[...] = jnp.sum(total, axis=0, keepdims=True)


def pass_kernel(
    round_index, heads_ref, relations_ref, ent_ref, *refs
):
    if round_index == 0:
        rel_rows = refs[0][...]
        refs = refs[1:]
    else:
        gradient = (refs[0][...] + refs[1][...])[:D, :]
        state = refs[3][...] + jnp.mean(gradient * gradient, axis=0, keepdims=True)
        rel_rows = refs[2][...] - gradient * (learn_rate * lax.rsqrt(state))
        rel_rows = rel_rows.astype(bf16).astype(f32)
        refs = refs[4:]
    tail_ref, neg_ref, band_ref, band_t_ref, bias_ref, fc_ref, fcb_ref = refs[:7]
    pack_out, head_out, tail_out, neg_out, picture, slopes, work, total = refs[7:]
    heads = heads_ref[round_index : round_index + 1, :]
    relations = relations_ref[round_index : round_index + 1, :]
    table = ent_ref[...].astype(bf16)
    picture[:D, :] = dot(table, hits(heads, table.shape[1]))
    picture[D:, :] = rel_rows
    number = LANES
    pre2 = jnp.zeros((number, D), f32)
    for pair in range(PAIRS):
        first = pair * 2 * EMB_W
        window = jnp.transpose(picture[first : first + WINDOW, :]).astype(bf16)
        pre1 = dot(window, band_ref[...]) + bias_ref[...]
        sigma = sigmoid(pre1)
        act = pre1 * sigma
        slopes[pair] = sigma + act * (1.0 - sigma)
        work[pair] = act.astype(bf16)
        pre2 = pre2 + dot(work[pair], fc_ref[pair])
    pre2 = pre2 + fcb_ref[...]
    sigma = sigmoid(pre2)
    value = pre2 * sigma
    slope2 = sigma + value * (1.0 - sigma)
    query = value.astype(bf16)
    query32 = query.astype(f32)
    tails = tail_ref[...].astype(f32)
    pos_grad = -sigmoid(-jnp.sum(query32 * tails, axis=1, keepdims=True))
    negset = neg_ref[...]
    neg_grad = (negative_weight * sigmoid(dot_nt(query, negset))).astype(bf16)
    query_grad = pos_grad * tails + dot(neg_grad, negset)
    pre2_grad = (query_grad * slope2).astype(bf16)
    tail_out[...] = jnp.transpose(pos_grad * query32)
    neg_out[...] = dot_tn(neg_grad, query)
    total[...] = jnp.zeros_like(total)
    for pair in range(PAIRS):
        act_grad = dot_nt(pre2_grad, fc_ref[pair])
        work[pair] = (act_grad * slopes[pair]).astype(bf16)
        part = dot(work[pair], band_t_ref[...])
        at = slice(pair * 2 * EMB_W, pair * 2 * EMB_W + WINDOW)
        total[at, :] = total[at, :] + jnp.transpose(part)[:WINDOW, :]
    head_out[...] = total[:D, :]
    high = relations >> 6
    low = relations - (high << 6)
    spare = lax.broadcasted_iota(i32, (PACK - D, number), 0)
    codes = jnp.where(spare == 0, high, jnp.where(spare == 1, low, 0)).astype(f32)
    pack_out[...] = jnp.concatenate([total[D:, :], codes], axis=0).astype(bf16)


def entity_kernel(
    round_index, heads_ref, asked_ref, next_ref, ent_ref, state_ref, head_ref, tail_ref, neg_ref, *outs
):
    count = ent_ref.shape[1]
    grads = jnp.concatenate([head_ref[...], tail_ref[...], turned(neg_ref[...])], axis=1)
    high, low = halves(grads)
    named = jnp.concatenate(
        [heads_ref[round_index : round_index + 1, :], asked_ref[0:1, :], asked_ref[1:2, :]], axis=1
    )
    both = dot_nt(jnp.concatenate([high, low], axis=0), hits(named, count))
    gradient = both[:D, :] + both[D:, :]
    state = state_ref[...] + jnp.mean(gradient * gradient, axis=0, keepdims=True)
    rows = ent_ref[...] - gradient * (learn_rate * lax.rsqrt(state))
    outs[0][...] = rows
    outs[1][...] = state
    if len(outs) > 2:
        pick_answer(rows.astype(bf16), next_ref, neg_ref.shape[0], outs[2])


def lay_packs(place_ref, mine_ref, other_ref, grads, names):
    half = mine_ref.shape[0]
    for index in range(2 * half):
        spot = place_ref[index]
        at = slice(index * LANES, (index + 1) * LANES)
        inner = lax.rem(spot, half)
        block = jnp.where(spot < half, mine_ref[inner].astype(f32), other_ref[inner].astype(f32))
        grads[:, at] = block.astype(bf16)
        names[0:1, at] = (block[D : D + 1, :] * 64.0 + block[D + 1 : D + 2, :]).astype(i32)


def need_kernel(round_index, place_ref, mine_ref, other_ref, ids_ref, others_ref, own_out, send_out, grads, names):
    lay_packs(place_ref, mine_ref, other_ref, grads, names)
    wide = names.shape[1]
    for ids, out in ((ids_ref, own_out), (others_ref, send_out)):
        column = as_column(ids[round_index : round_index + 1, :])
        hit = jnp.concatenate(
            [
                jnp.where(
                    column == names[0:1, at : at + LANES].astype(f32), 1.0, 0.0
                ).astype(bf16)
                for at in range(0, wide, LANES)
            ],
            axis=1,
        )
        out[...] = jnp.transpose(dot_nt(hit, grads[...]))


def sums_kernel(place_ref, mine_ref, other_ref, out, grads, names):
    lay_packs(place_ref, mine_ref, other_ref, grads, names)
    for first in range(0, out.shape[1], LANES):
        out[:, first : first + LANES] = dot_nt(grads[...], hits(names[0:1, :], LANES, first))[:D, :]


def relation_kernel(rel_ref, state_ref, *refs):
    rows = rel_ref[...]
    state = state_ref[...]
    count = rows.shape[1]
    for index in range(ROUNDS):
        gradient = refs[2 * index][:, :count] + refs[2 * index + 1][:, :count]
        state = state + jnp.mean(gradient * gradient, axis=0, keepdims=True)
        rows = rows - gradient * (learn_rate * lax.rsqrt(state))
    refs[2 * ROUNDS][...] = rows
    refs[2 * ROUNDS + 1][...] = state


def swapped(bits):
    out = list(bits)
    for index in range(0, len(out) - 1, 2):
        out[index], out[index + 1] = out[index + 1], out[index]
    return out


class Plan:
    def __init__(self, groups, shards):
        self.total = groups * shards
        self.shards = shards
        near = [1 << bit for bit in range(1, shards.bit_length() - 1)]
        far = [shards << bit for bit in range(groups.bit_length() - 1)]
        self.even = near + far
        self.odd = swapped(near) + swapped(far)
        self.across = [self.route(a, b) for a, b in zip(self.even, self.odd)]
        self.core = self.route(1, 1)
        self.within = self.across[: len(near)] + [self.core]

    def route(self, even, odd):
        return [(at, at ^ (odd if at & 1 else even)) for at in range(self.total)]

    def partner(self, bit):
        mask = self.shards << bit
        return self.route(mask, mask)

    def places(self, me):
        source = jnp.arange(0, self.total, 2, dtype=i32)
        differ = source ^ me
        even = jnp.zeros_like(source)
        odd = jnp.zeros_like(source)
        for step, (one, other) in enumerate(zip(self.even, self.odd)):
            even = even + jnp.where((differ & one) != 0, 1 << step, 0)
            odd = odd + jnp.where((differ & other) != 0, 1 << step, 0)
        return jnp.where((me & 1) == 0, even, odd)


def send(block, route):
    return lax.ppermute(block, BOTH, route)


def doubled(block, routes):
    for route in routes:
        block = jnp.concatenate([block, send(block, route)], axis=0)
    return block


def halved(block, routes):
    for route in reversed(routes):
        half = block.shape[0] // 2
        block = block[:half] + send(block[half:], route)
    return block


def shards(
    plan,
    entity_rows,
    entity_state,
    relation_rows,
    relation_state,
    conv_weight,
    conv_bias,
    fc_weight,
    fc_bias,
    head_ids,
    rel_ids,
    tail_ids,
    neg_ids,
):
    number = head_ids.shape[1]
    negatives = neg_ids.shape[1]
    count = relation_rows.shape[0]
    wide = count + -count % LANES
    sources = plan.total // 2
    me = lax.axis_index("group") * plan.shards + lax.axis_index("shard")
    ent = entity_rows.T
    ent_state = entity_state[None, :]
    rel = relation_rows.T
    rel_state = relation_state[None, :]

    wanted = call(
        wanted_kernel, "wanted", 1, [shaped((2, LANES), i32)] * ROUNDS, (tail_ids, neg_ids)
    )
    requested = [send(wanted[r], plan.partner(r)) for r in range(ROUNDS)]
    rel_others = send(rel_ids, plan.core)
    answer_shape = shaped((number + negatives, D), bf16)
    (answer,) = call(
        functools.partial(answer_kernel, negatives), "answer", 1, [answer_shape], (requested[0], ent)
    )
    taps = jnp.tile(conv_weight.reshape(FILTERS, 9).T.astype(f32), (1, WIDE // FILTERS))
    bias = jnp.tile(conv_bias[None, :], (1, WIDE // FILTERS))
    features = fc_weight.shape[0]
    fc, band, band_t = call(
        prepare_kernel,
        "prepare",
        5,
        [shaped((features, D), bf16), shaped((WINDOW, WIDE), bf16), shaped((WIDE, LANES), bf16)],
        (fc_weight.T, taps),
        [pltpu.VMEM((features, LANES), f32), pltpu.VMEM((features, LANES), f32)],
    )
    fc = fc.reshape(PAIRS, WIDE, D)
    rel_first, rel_later, state_later = call(
        rows_kernel,
        "relation_rows",
        2,
        [shaped((D, number)), shaped((D, number)), shaped((1, number))],
        (rel_ids, rel, rel_state),
        [pltpu.VMEM((D, wide), f32)],
    )
    rel_inputs = (rel_first,)
    place = plan.places(me)
    lay = [pltpu.VMEM((PACK, sources * LANES), bf16), pltpu.VMEM((8, sources * LANES), i32)]

    sums = []
    for r in range(ROUNDS):
        last = r == ROUNDS - 1
        answered = send(answer, plan.partner(r))
        negset = doubled(answered[number:], plan.within)
        pack, head_grad, tail_grad, neg_part = call(
            functools.partial(pass_kernel, r),
            "local_pass",
            6,
            [
                shaped((PACK, number), bf16),
                shaped((D, number)),
                shaped((D, number)),
                shaped((negset.shape[0], D)),
            ],
            (head_ids, rel_ids, ent, *rel_inputs, answered[:number], negset, band, band_t, bias, fc, fc_bias[None, :]),
            [
                pltpu.VMEM((PIXELS, number), f32),
                pltpu.VMEM((PAIRS, number, WIDE), f32),
                pltpu.VMEM((PAIRS, number, WIDE), bf16),
                pltpu.VMEM((PIXELS, number), f32),
            ],
        )
        packs = doubled(pack[None], plan.across[:-1])
        arrived = send(packs, plan.across[-1])
        tail_back = send(tail_grad, plan.partner(r))
        neg_back = send(halved(neg_part, plan.within), plan.partner(r))
        if not last:
            own, partial = call(
                functools.partial(need_kernel, r + 1),
                "need",
                1.5,
                [shaped((PACK, number))] * 2,
                (place, packs, arrived, rel_ids, rel_others),
                lay,
                scalars=1,
            )
            rel_inputs = (own, send(partial, plan.core), rel_later, state_later)
        out_shape = [shaped(ent.shape), shaped(ent_state.shape)]
        outs = call(
            functools.partial(entity_kernel, r),
            "entity_update",
            2,
            out_shape if last else out_shape + [answer_shape],
            (head_ids, requested[r], requested[min(r + 1, ROUNDS - 1)], ent, ent_state, head_grad, tail_back, neg_back),
        )
        ent, ent_state = outs[:2]
        if not last:
            answer = outs[2]
        (part,) = call(
            sums_kernel, "relation_sums", 3, [shaped((D, wide))], (place, packs, arrived), lay, scalars=1
        )
        sums += [part, send(part, plan.core)]
    rel, rel_state = call(
        relation_kernel, "relation_update", 2, [shaped((D, count)), shaped((1, count))], (rel, rel_state, *sums)
    )
    return (ent.T, ent_state.reshape(-1), rel.T, rel_state.reshape(-1))


def solution(mesh):
    plan = Plan(mesh.shape["group"], mesh.shape["shard"])
    in_specs = (
        P(BOTH, None),
        P(BOTH),
        P(),
        P(),
        P(),
        P(),
        P(),
        P(),
        P(None, BOTH),
        P(None, BOTH),
        P(None, BOTH),
        P(None, BOTH),
    )
    out_specs = (P(BOTH, None), P(BOTH), P(), P())
    return jax.shard_map(
        functools.partial(shards, plan),
        mesh=mesh,
        in_specs=in_specs,
        out_specs=out_specs,
        check_vma=False,
    )
```

```python
import functools

import jax
import jax.numpy as jnp
from jax import lax
from jax.experimental import pallas as pl
from jax.experimental.pallas import tpu as pltpu
from jax.sharding import PartitionSpec as P

EMB_W = 20
D = 200
FILTERS = 32
PIXELS = 400
SIDE = 18
PAIRS = 9
WINDOW = 80
WIDE = 1152
PACK = 208
LANES = 128
ROUNDS = 2

negative_weight = 0.03125
learn_rate = 0.5

f32 = jnp.float32
bf16 = jnp.bfloat16
i32 = jnp.int32
BOTH = ("group", "shard")
VMEM = pl.BlockSpec(memory_space=pltpu.VMEM)
SMEM = pl.BlockSpec(memory_space=pltpu.SMEM)


def shaped(shape, dtype=f32):
    return jax.ShapeDtypeStruct(shape, dtype)


def call(kernel, name, micros, out_shape, args, scratch=(), scalars=0, limit=16):
    return pl.pallas_call(
        kernel,
        out_shape=out_shape,
        in_specs=[SMEM] * scalars + [VMEM] * (len(args) - scalars),
        out_specs=[VMEM] * len(out_shape),
        scratch_shapes=list(scratch),
        compiler_params=pltpu.CompilerParams(vmem_limit_bytes=limit * 1024 * 1024),
        cost_estimate=pl.CostEstimate(
            flops=int(micros * 1e9), bytes_accessed=int(micros * 3e6), transcendentals=0
        ),
        name=name,
    )(*args)


def sigmoid(values):
    return 0.5 * jnp.tanh(0.5 * values) + 0.5


def dot(left, right):
    return jnp.dot(left, right, preferred_element_type=f32)


def dot_nt(left, right):
    return lax.dot_general(left, right, (((1,), (1,)), ((), ())), preferred_element_type=f32)


def dot_tn(left, right):
    return lax.dot_general(left, right, (((0,), (0,)), ((), ())), preferred_element_type=f32)


def as_column(row):
    return jnp.transpose(jnp.broadcast_to(row.astype(f32), (LANES, LANES)))


def hits(names_row, count, first=0):
    spot = lax.broadcasted_iota(i32, (count, names_row.shape[1]), 0) + first
    return jnp.where(spot == names_row, 1.0, 0.0).astype(bf16)


def halves(values):
    high = values.astype(bf16)
    return high, (values - high.astype(f32)).astype(bf16)


def padded(values, lanes):
    rest = lanes - values.shape[1]
    return jnp.concatenate([values, jnp.zeros((values.shape[0], rest), values.dtype)], axis=1)


def turned(values):
    rest = -values.shape[0] % LANES
    return jnp.transpose(jnp.concatenate([values, jnp.zeros((rest, D), f32)], axis=0))


def wanted_kernel(tails_ref, negatives_ref, *outs):
    for index, out in enumerate(outs):
        out[0:1, :] = tails_ref[index : index + 1, :]
        out[1:2, :] = padded(negatives_ref[index : index + 1, :], LANES)


def pick_answer(table, ids_ref, negatives, out):
    count = table.shape[1]
    number = out.shape[0] - negatives
    tails = dot(table, hits(ids_ref[0:1, :], count))
    out[:number, :] = jnp.transpose(tails).astype(bf16)
    negs = dot(table, hits(ids_ref[1:2, :], count))
    out[number:, :] = jnp.transpose(negs)[:negatives, :].astype(bf16)


def answer_kernel(negatives, ids_ref, ent_ref, out):
    pick_answer(ent_ref[...].astype(bf16), ids_ref, negatives, out)


def prepare_kernel(fc_ref, taps_ref, fc_out, band_out, band_t_out, left, right):
    blank = jnp.zeros((2 * LANES - D, LANES), f32)
    for index in range(fc_ref.shape[1] // LANES):
        at = slice(index * LANES, (index + 1) * LANES)
        block = fc_ref[:, at].astype(f32)
        left[at, :] = jnp.transpose(block[:LANES])
        right[at, :] = jnp.transpose(jnp.concatenate([block[LANES:], blank], axis=0))
    spots = SIDE * SIDE

    def regroup(index, carry):
        low = left[pl.ds(index, FILTERS, stride=spots), :]
        high = right[pl.ds(index, FILTERS, stride=spots), :]
        at = pl.ds(pl.multiple_of(index * FILTERS, FILTERS), FILTERS)
        fc_out[at, :LANES] = low.astype(bf16)
        fc_out[at, LANES:] = high[:, : D - LANES].astype(bf16)
        return carry

    lax.fori_loop(0, spots, regroup, 0, unroll=9)
    group = lax.broadcasted_iota(i32, (WINDOW, WIDE), 1) >> 5
    start = group + jnp.where(group >= SIDE, EMB_W - SIDE, 0)
    gap = lax.broadcasted_iota(i32, (WINDOW, WIDE), 0) - start
    band = jnp.zeros((WINDOW, WIDE), f32)
    for row_off in range(3):
        for col_off in range(3):
            tap = row_off * 3 + col_off
            hit = gap == EMB_W * row_off + col_off
            band = jnp.where(hit, taps_ref[tap : tap + 1, :], band)
    band_out[...] = band.astype(bf16)
    band_t_out[...] = jnp.transpose(
        jnp.concatenate([band, jnp.zeros((LANES - WINDOW, WIDE), f32)], axis=0)
    ).astype(bf16)


def rows_kernel(ids_ref, rel_ref, state_ref, first_out, later_out, state_out, table):
    count = rel_ref.shape[1]
    whole = count // LANES * LANES
    table[:, :whole] = rel_ref[:, :whole]
    rest = jnp.concatenate(
        [rel_ref[:, whole:], jnp.zeros((D, LANES - count + whole), f32)], axis=1
    )
    table[:, whole:] = rest
    values = table[...]
    wide = values.shape[1]
    high = values.astype(bf16)
    first_out[...] = dot(high, hits(ids_ref[0:1, :], wide))
    left = values - high.astype(f32)
    middle = left.astype(bf16)
    low = (left - middle.astype(f32)).astype(bf16)
    hit = hits(ids_ref[1:2, :], wide)
    later_out[...] = dot(high, hit) + dot(middle, hit) + dot(low, hit)
    sums = padded(state_ref[...], wide)
    names = ids_ref[1:2, :]
    total = jnp.zeros((LANES, LANES), f32)
    for block in range(wide // LANES):
        states = as_column(sums[:, block * LANES : (block + 1) * LANES])
        spot = lax.broadcasted_iota(i32, (LANES, LANES), 0) + block * LANES
        total = total + jnp.where(spot == names, states, 0.0)
    state_out[...] = jnp.sum(total, axis=0, keepdims=True)


def forward_kernel(round_index, heads_ref, ent_ref, *refs):
    if round_index == 0:
        rel_rows = refs[0][...]
        refs = refs[1:]
    else:
        gradient = (refs[0][...] + refs[1][...])[:D, :]
        state = refs[3][...] + jnp.mean(gradient * gradient, axis=0, keepdims=True)
        rel_rows = refs[2][...] - gradient * (learn_rate * lax.rsqrt(state))
        rel_rows = rel_rows.astype(bf16).astype(f32)
        refs = refs[4:]
    band_ref, bias_ref, fc_ref, fcb_ref, pre2_out, slopes, picture, work = refs
    heads = heads_ref[round_index : round_index + 1, :]
    table = ent_ref[...].astype(bf16)
    picture[:D, :] = dot(table, hits(heads, table.shape[1]))
    picture[D:, :] = rel_rows
    pre2 = jnp.zeros(pre2_out.shape, f32)
    for pair in range(PAIRS):
        first = pair * 2 * EMB_W
        window = jnp.transpose(picture[first : first + WINDOW, :]).astype(bf16)
        pre1 = dot(window, band_ref[...]) + bias_ref[...]
        sigma = sigmoid(pre1)
        act = pre1 * sigma
        slopes[pair] = sigma + act * (1.0 - sigma)
        work[pair] = act.astype(bf16)
        pre2 = pre2 + dot(work[pair], fc_ref[pair])
    pre2_out[...] = pre2 + fcb_ref[...]


def score_kernel(pre2_ref, tail_ref, neg_ref, grad_out, tail_out, neg_out):
    pre2 = pre2_ref[...]
    sigma = sigmoid(pre2)
    value = pre2 * sigma
    slope = sigma + value * (1.0 - sigma)
    query = value.astype(bf16)
    query32 = query.astype(f32)
    tails = tail_ref[...].astype(f32)
    pos_grad = -sigmoid(-jnp.sum(query32 * tails, axis=1, keepdims=True))
    negset = neg_ref[...]
    neg_grad = (negative_weight * sigmoid(dot_nt(query, negset))).astype(bf16)
    query_grad = pos_grad * tails + dot(neg_grad, negset)
    grad_out[...] = (query_grad * slope).astype(bf16)
    tail_out[...] = pos_grad * query32
    neg_out[...] = dot_tn(neg_grad, query)


def backward_kernel(round_index, relations_ref, grad_ref, slopes, band_t_ref, fc_ref, pack_out, head_out, work, total):
    pre2_grad = grad_ref[...]
    total[...] = jnp.zeros_like(total)
    for pair in range(PAIRS):
        act_grad = dot_nt(pre2_grad, fc_ref[pair])
        work[pair] = (act_grad * slopes[pair]).astype(bf16)
        part = dot(work[pair], band_t_ref[...])
        at = slice(pair * 2 * EMB_W, pair * 2 * EMB_W + WINDOW)
        total[at, :] = total[at, :] + jnp.transpose(part)[:WINDOW, :]
    head_out[...] = total[:D, :]
    relations = relations_ref[round_index : round_index + 1, :]
    high = relations >> 6
    low = relations - (high << 6)
    spare = lax.broadcasted_iota(i32, (PACK - D, LANES), 0)
    codes = jnp.where(spare == 0, high, jnp.where(spare == 1, low, 0)).astype(f32)
    pack_out[...] = jnp.concatenate([total[D:, :], codes], axis=0).astype(bf16)


def entity_kernel(
    round_index, negatives, heads_ref, asked_ref, next_ref, ent_ref, state_ref, head_ref, back_ref, other_ref, *outs
):
    count = ent_ref.shape[1]
    number = back_ref.shape[0] - negatives
    back = jnp.concatenate([back_ref[:number, :], back_ref[number:, :] + other_ref[...]], axis=0)
    grads = jnp.concatenate([head_ref[...], turned(back)], axis=1)
    high, low = halves(grads)
    named = jnp.concatenate(
        [heads_ref[round_index : round_index + 1, :], asked_ref[0:1, :], asked_ref[1:2, :]], axis=1
    )
    both = dot_nt(jnp.concatenate([high, low], axis=0), hits(named, count))
    gradient = both[:D, :] + both[D:, :]
    state = state_ref[...] + jnp.mean(gradient * gradient, axis=0, keepdims=True)
    rows = ent_ref[...] - gradient * (learn_rate * lax.rsqrt(state))
    outs[0][...] = rows
    outs[1][...] = state
    if len(outs) > 2:
        pick_answer(rows.astype(bf16), next_ref, negatives, outs[2])


def lay_packs(place_ref, groups, grads, names):
    index = 0
    for group in groups:
        for inner in range(group.shape[0]):
            at = slice(index * LANES, (index + 1) * LANES)
            block = group[place_ref[inner]]
            grads[:, at] = block
            codes = block[PACK - 16 :, :].astype(f32)[D - PACK + 16 :, :]
            names[0:1, at] = (codes[0:1, :] * 64.0 + codes[1:2, :]).astype(i32)
            index += 1


def need_kernel(round_index, place_ref, *refs):
    groups, (ids_ref, others_ref, own_out, send_out, grads, names) = refs[:4], refs[4:]
    lay_packs(place_ref, groups, grads, names)
    wide = names.shape[1]
    for ids, out in ((others_ref, send_out), (ids_ref, own_out)):
        column = as_column(ids[round_index : round_index + 1, :])
        hit = jnp.concatenate(
            [
                jnp.where(
                    column == names[0:1, at : at + LANES].astype(f32), 1.0, 0.0
                ).astype(bf16)
                for at in range(0, wide, LANES)
            ],
            axis=1,
        )
        out[...] = jnp.transpose(dot_nt(hit, grads[...]))


def sums_kernel(kinds, place_ref, *refs):
    packs, before, refs = refs[: kinds[0]], refs[kinds[0] : sum(kinds)], refs[sum(kinds) :]
    outs, grads, names = refs[:-2], refs[-2], refs[-1]
    lay_packs(place_ref, packs, grads, names)
    size = names.shape[1] // len(packs)
    for first in range(0, outs[0].shape[1], LANES):
        at = slice(first, first + LANES)
        hit = hits(names[0:1, :], LANES, first)
        parts = [
            dot_nt(grads[:, k * size : (k + 1) * size], hit[:, k * size : (k + 1) * size])[:D, :]
            for k in range(len(packs))
        ]
        if len(packs) == 4:
            outs[0][:, at] = (parts[0] + parts[1]) + (parts[2] + parts[3])
        elif len(packs) == 3:
            outs[0][:, at] = parts[0] + parts[1]
            outs[1][:, at] = parts[2]
        else:
            outs[0][:, at] = before[0][:, at] + (before[1][:, at] + parts[0])


def relation_kernel(rel_ref, state_ref, *refs):
    rows = rel_ref[...]
    state = state_ref[...]
    count = rows.shape[1]
    for index in range(ROUNDS):
        gradient = refs[2 * index][:, :count] + refs[2 * index + 1][:, :count]
        state = state + jnp.mean(gradient * gradient, axis=0, keepdims=True)
        rows = rows - gradient * (learn_rate * lax.rsqrt(state))
    refs[2 * ROUNDS][...] = rows
    refs[2 * ROUNDS + 1][...] = state


class Plan:
    def __init__(self, groups, shards):
        self.total = groups * shards
        self.shards = shards
        self.near = [1 << bit for bit in range(1, shards.bit_length() - 1)]
        self.far = [shards << bit for bit in range(groups.bit_length() - 1)]
        self.lead = self.near + self.far[:-2]

    def route(self, mask):
        return [(at, at ^ mask) for at in range(self.total)]

    def partner(self, bit):
        return self.shards << bit

    def send(self, block, mask):
        return lax.ppermute(block, BOTH, self.route(mask))

    def places(self, me):
        mine = sum(((me & mask) != 0).astype(i32) << step for step, mask in enumerate(self.lead))
        return jnp.arange(1 << len(self.lead), dtype=i32) ^ mine


def together(*values):
    return lax.optimization_barrier(values)


def shards(
    plan,
    entity_rows,
    entity_state,
    relation_rows,
    relation_state,
    conv_weight,
    conv_bias,
    fc_weight,
    fc_bias,
    head_ids,
    rel_ids,
    tail_ids,
    neg_ids,
):
    number = head_ids.shape[1]
    negatives = neg_ids.shape[1]
    count = relation_rows.shape[0]
    wide = count + -count % LANES
    features = fc_weight.shape[0]
    group = 1 << len(plan.lead)
    send = plan.send
    me = lax.axis_index("group") * plan.shards + lax.axis_index("shard")
    place = plan.places(me)
    ent = entity_rows.T
    ent_state = entity_state[None, :]
    rel = relation_rows.T
    rel_state = relation_state[None, :]
    bias2 = fc_bias[None, :]
    next_door, beyond = plan.near[0], plan.near[1:]

    def asked_rows(answer, bit):
        near = send(answer, plan.partner(bit))
        side = send(answer[number:], plan.partner(bit) | next_door)
        return near, side

    wanted = call(
        wanted_kernel, "wanted", 1, [shaped((2, LANES), i32)] * ROUNDS, (tail_ids, neg_ids)
    )
    requested = [send(wanted[0], plan.partner(0))]
    answer_shape = shaped((number + negatives, D), bf16)
    (answer,) = call(
        functools.partial(answer_kernel, negatives), "answer", 1, [answer_shape], (requested[0], ent)
    )
    rel_first, rel_later, state_later = call(
        rows_kernel,
        "relation_rows",
        1,
        [shaped((D, number)), shaped((D, number)), shaped((1, number))],
        (rel_ids, rel, rel_state),
        [pltpu.VMEM((D, wide), f32)],
    )
    near, side = asked_rows(answer, 0)
    near, side, rel_first, rel_later, state_later = together(
        near, side, rel_first, rel_later, state_later
    )
    negset = jnp.concatenate([near[number:], side], axis=0)
    taps = jnp.tile(conv_weight.reshape(FILTERS, 9).T.astype(f32), (1, WIDE // FILTERS))
    bias = jnp.tile(conv_bias[None, :], (1, WIDE // FILTERS))
    fc, band, band_t = call(
        prepare_kernel,
        "prepare",
        4,
        [shaped((features, D), bf16), shaped((WINDOW, WIDE), bf16), shaped((WIDE, LANES), bf16)],
        (fc_weight.T, taps),
        [pltpu.VMEM((features, LANES), f32), pltpu.VMEM((features, LANES), f32)],
        limit=24,
    )
    fc = fc.reshape(PAIRS, WIDE, D)
    for mask in beyond:
        negset = jnp.concatenate([negset, send(negset, mask)], axis=0)
    near, negset, fc, band, band_t = together(near, negset, fc, band, band_t)
    requested.append(send(wanted[1], plan.partner(1)))
    rel_others = send(rel_ids, 1)
    negset = jnp.concatenate([negset, send(negset, 1)], axis=0)
    rel_inputs = (rel_first,)

    def lay(sources):
        return [pltpu.VMEM((PACK, sources * LANES), bf16), pltpu.VMEM((8, sources * LANES), i32)]

    sums = []
    for r in range(ROUNDS):
        last = r == ROUNDS - 1
        pre2, slopes = call(
            functools.partial(forward_kernel, r),
            "forward",
            2.5,
            [shaped((number, D)), shaped((PAIRS, number, WIDE))],
            (head_ids, ent, *rel_inputs, band, bias, fc, bias2),
            [pltpu.VMEM((PIXELS, number), f32), pltpu.VMEM((PAIRS, number, WIDE), bf16)],
            limit=24,
        )
        grad2, tail_grad, neg_part = call(
            score_kernel,
            "scores",
            1,
            [shaped((number, D), bf16), shaped((number, D)), shaped((negset.shape[0], D))],
            (pre2, near[:number], negset),
        )
        if r == 0:
            grad2, neg_part, requested[1], rel_others = together(
                grad2, neg_part, requested[1], rel_others
            )
        half = neg_part.shape[0] // 2
        arrived = send(neg_part[half:], 1)
        pack, head_grad = call(
            functools.partial(backward_kernel, r),
            "backward",
            3,
            [shaped((PACK, number), bf16), shaped((D, number))],
            (rel_ids, grad2, slopes, band_t, fc),
            [pltpu.VMEM((PAIRS, number, WIDE), bf16), pltpu.VMEM((PIXELS, number), f32)],
            limit=24,
        )
        pack, arrived = together(pack, arrived)
        share = neg_part[:half] + arrived
        packs = pack[None]
        lead = list(plan.lead)
        back = list(reversed(beyond))
        for step, mask in enumerate(lead):
            came = send(packs, mask)
            if step < len(back):
                half = share.shape[0] // 2
                arrived = send(share[half:], back[step])
                came, arrived = together(came, arrived)
                share = share[:half] + arrived
            elif step == len(lead) - 1:
                own_back = jnp.concatenate([tail_grad, share[:negatives]], axis=0)
                to_owner = send(own_back, plan.partner(r))
                to_side = send(share[negatives:], plan.partner(r) | next_door)
                came, to_owner, to_side = together(came, to_owner, to_side)
            packs = jnp.concatenate([packs, came], axis=0)
            if last and step == 0:
                (part,) = call(
                    functools.partial(sums_kernel, (4, 0)),
                    "relation_sums",
                    3,
                    [shaped((D, wide))],
                    (place, *groups),
                    lay(4 * group),
                    scalars=1,
                )
                packs, part = together(packs, part)
                sums = [part, send(part, 1)]
        one, other = plan.far[-2:]
        across = send(packs, one)
        along = send(packs, other)
        out_shape = [shaped(ent.shape), shaped(ent_state.shape)]
        outs = call(
            functools.partial(entity_kernel, r, negatives),
            "entity_update",
            1.5,
            out_shape if last else out_shape + [answer_shape],
            (
                head_ids,
                requested[r],
                requested[min(r + 1, ROUNDS - 1)],
                ent,
                ent_state,
                head_grad,
                to_owner,
                to_side,
            ),
        )
        ent, ent_state = outs[:2]
        if last:
            across, along, ent, ent_state, *sums = together(across, along, ent, ent_state, *sums)
            corner = send(across, other)
            early = call(
                functools.partial(sums_kernel, (3, 0)),
                "early_sums",
                3,
                [shaped((D, wide))] * 2,
                (place, packs, across, along),
                lay(3 * group),
                scalars=1,
            )
            corner, *early = together(corner, *early)
            (part,) = call(
                functools.partial(sums_kernel, (1, 2)),
                "late_sums",
                1,
                [shaped((D, wide))],
                (place, corner, *early),
                lay(group),
                scalars=1,
            )
            sums += [part, send(part, 1)]
        else:
            near, side = asked_rows(outs[2], r + 1)
            corner = send(across, other)
            groups = (packs, across, along, corner)
            near, side = together(near, side)
            negset = jnp.concatenate([near[number:], side], axis=0)
            for mask in beyond:
                negset = jnp.concatenate([negset, send(negset, mask)], axis=0)
            own, partial = call(
                functools.partial(need_kernel, r + 1),
                "need",
                1.5,
                [shaped((PACK, number))] * 2,
                (place, *groups, rel_ids, rel_others),
                lay(4 * group),
                scalars=1,
            )
            negset, own, partial = together(negset, own, partial)
            rel_inputs = (own, send(partial, 1), rel_later, state_later)
            negset = jnp.concatenate([negset, send(negset, 1)], axis=0)
    rel, rel_state = call(
        relation_kernel, "relation_update", 2, [shaped((D, count)), shaped((1, count))], (rel, rel_state, *sums)
    )
    return (ent.T, ent_state.reshape(-1), rel.T, rel_state.reshape(-1))


def solution(mesh):
    plan = Plan(mesh.shape["group"], mesh.shape["shard"])
    in_specs = (
        P(BOTH, None),
        P(BOTH),
        P(),
        P(),
        P(),
        P(),
        P(),
        P(),
        P(None, BOTH),
        P(None, BOTH),
        P(None, BOTH),
        P(None, BOTH),
    )
    out_specs = (P(BOTH, None), P(BOTH), P(), P())
    return jax.shard_map(
        functools.partial(shards, plan),
        mesh=mesh,
        in_specs=in_specs,
        out_specs=out_specs,
        check_vma=False,
    )
```

```python
import functools

import jax
import jax.numpy as jnp
from jax import lax
from jax.experimental import pallas as pl
from jax.experimental.pallas import tpu as pltpu
from jax.sharding import PartitionSpec as P

EMB_W = 20
D = 200
FILTERS = 32
PIXELS = 400
SIDE = 18
PAIRS = 9
WINDOW = 80
WIDE = 1152
PACK = 208
LANES = 128
ROUNDS = 2
LIM = 24
LIMP = 28

negative_weight = 0.03125
learn_rate = 0.5

f32 = jnp.float32
bf16 = jnp.bfloat16
i32 = jnp.int32
BOTH = ("group", "shard")
VMEM = pl.BlockSpec(memory_space=pltpu.VMEM)
SMEM = pl.BlockSpec(memory_space=pltpu.SMEM)
HBM = pl.BlockSpec(memory_space=pltpu.HBM)


def shaped(shape, dtype=f32):
    return jax.ShapeDtypeStruct(shape, dtype)


def call(kernel, name, micros, out_shape, args, scratch=(), scalars=0, limit=16, far=(), near=(), near_out=(), alias=None):
    places = [SMEM] * scalars + [VMEM] * (len(args) - scalars)
    args = [
        pltpu.with_memory_space_constraint(arg, pltpu.HBM)
        if index in far
        else pltpu.with_memory_space_constraint(arg, pltpu.VMEM)
        if index in near
        else arg
        for index, arg in enumerate(args)
    ]
    return pl.pallas_call(
        kernel,
        out_shape=[
            pltpu.VMEM(out.shape, out.dtype) if index in near_out else out
            for index, out in enumerate(out_shape)
        ],
        input_output_aliases=alias or {},
        in_specs=[HBM if index in far else spec for index, spec in enumerate(places)],
        out_specs=[VMEM] * len(out_shape),
        scratch_shapes=list(scratch),
        compiler_params=pltpu.CompilerParams(vmem_limit_bytes=limit * 1024 * 1024),
        cost_estimate=pl.CostEstimate(
            flops=int(micros * 1e9), bytes_accessed=int(micros * 3e6), transcendentals=0
        ),
        name=name,
    )(*args)


def sigmoid(values):
    return 0.5 * jnp.tanh(0.5 * values) + 0.5


def dot(left, right):
    return jnp.dot(left, right, preferred_element_type=f32)


def dot_nt(left, right):
    return lax.dot_general(left, right, (((1,), (1,)), ((), ())), preferred_element_type=f32)


def dot_tn(left, right):
    return lax.dot_general(left, right, (((0,), (0,)), ((), ())), preferred_element_type=f32)


def as_column(row):
    return jnp.transpose(jnp.broadcast_to(row.astype(f32), (LANES, LANES)))


def hits(names_row, count, first=0):
    spot = lax.broadcasted_iota(i32, (count, names_row.shape[1]), 0) + first
    return jnp.where(spot == names_row, 1.0, 0.0).astype(bf16)


def halves(values):
    high = values.astype(bf16)
    return high, (values - high.astype(f32)).astype(bf16)


def padded(values, lanes):
    rest = lanes - values.shape[1]
    return jnp.concatenate([values, jnp.zeros((values.shape[0], rest), values.dtype)], axis=1)


def turned(values):
    rest = -values.shape[0] % LANES
    return jnp.transpose(jnp.concatenate([values, jnp.zeros((rest, D), f32)], axis=0))


def wanted_kernel(tails_hbm, negatives_hbm, *refs):
    outs, (tails_ref, negatives_ref, sems) = refs[:ROUNDS], refs[ROUNDS:]
    copies = [
        pltpu.make_async_copy(tails_hbm, tails_ref, sems.at[0]),
        pltpu.make_async_copy(negatives_hbm, negatives_ref, sems.at[1]),
    ]
    for copy in copies:
        copy.start()
    for copy in copies:
        copy.wait()
    for index, out in enumerate(outs):
        out[0:1, :] = tails_ref[index : index + 1, :]
        out[1:2, :] = padded(negatives_ref[index : index + 1, :], LANES)


def pick_answer(table, ids_ref, negatives, out):
    count = table.shape[1]
    number = out.shape[0] - negatives
    tails = dot(table, hits(ids_ref[0:1, :], count))
    out[:number, :] = jnp.transpose(tails).astype(bf16)
    negs = dot(table, hits(ids_ref[1:2, :], count))
    out[number:, :] = jnp.transpose(negs)[:negatives, :].astype(bf16)


def answer_kernel(negatives, ids_ref, ent_ref, out):
    pick_answer(ent_ref[...].astype(bf16), ids_ref, negatives, out)


def prepare(fc_hbm, taps_ref, band_out, band_t_out, fc_ref, sems, left, right):
    copies = []
    for pair in range(PAIRS):
        at = pl.ds(pair * WIDE, WIDE)
        copies.append(pltpu.make_async_copy(fc_hbm.at[:, at], fc_ref.at[:, at], sems.at[pair]))
        copies[-1].start()
    group = lax.broadcasted_iota(i32, (WINDOW, WIDE), 1) >> 5
    start = group + jnp.where(group >= SIDE, EMB_W - SIDE, 0)
    gap = lax.broadcasted_iota(i32, (WINDOW, WIDE), 0) - start
    band = jnp.zeros((WINDOW, WIDE), f32)
    for row_off in range(3):
        for col_off in range(3):
            tap = row_off * 3 + col_off
            hit = gap == EMB_W * row_off + col_off
            band = jnp.where(hit, taps_ref[tap : tap + 1, :], band)
    band_out[...] = band.astype(bf16)
    band_t_out[...] = jnp.transpose(
        jnp.concatenate([band, jnp.zeros((LANES - WINDOW, WIDE), f32)], axis=0)
    ).astype(bf16)
    for copy in copies:
        copy.wait()
    blank = jnp.zeros((2 * LANES - D, LANES), f32)
    for index in range(fc_ref.shape[1] // LANES):
        at = slice(index * LANES, (index + 1) * LANES)
        block = fc_ref[:, at].astype(f32)
        left[at, :] = jnp.transpose(block[:LANES])
        right[at, :] = jnp.transpose(jnp.concatenate([block[LANES:], blank], axis=0))


def regroup(pair, fc_out, left, right):
    spots = SIDE * SIDE
    each = spots // PAIRS
    for index in range(each):
        low = left[pl.ds(pair * each + index, FILTERS, stride=spots), :]
        high = right[pl.ds(pair * each + index, FILTERS, stride=spots), :]
        at = slice(index * FILTERS, (index + 1) * FILTERS)
        fc_out[pair, at, :LANES] = low.astype(bf16)
        fc_out[pair, at, LANES:] = high[:, : D - LANES].astype(bf16)


def rows_kernel(ids_ref, rel_ref, state_ref, first_out, later_out, state_out, table):
    count = rel_ref.shape[1]
    whole = count // LANES * LANES
    table[:, :whole] = rel_ref[:, :whole]
    rest = jnp.concatenate(
        [rel_ref[:, whole:], jnp.zeros((D, LANES - count + whole), f32)], axis=1
    )
    table[:, whole:] = rest
    values = table[...]
    wide = values.shape[1]
    high = values.astype(bf16)
    first_out[...] = dot(high, hits(ids_ref[0:1, :], wide))
    left = values - high.astype(f32)
    middle = left.astype(bf16)
    low = (left - middle.astype(f32)).astype(bf16)
    hit = hits(ids_ref[1:2, :], wide)
    later_out[...] = dot(high, hit) + dot(middle, hit) + dot(low, hit)
    sums = padded(state_ref[...], wide)
    names = ids_ref[1:2, :]
    total = jnp.zeros((LANES, LANES), f32)
    for block in range(wide // LANES):
        states = as_column(sums[:, block * LANES : (block + 1) * LANES])
        spot = lax.broadcasted_iota(i32, (LANES, LANES), 0) + block * LANES
        total = total + jnp.where(spot == names, states, 0.0)
    state_out[...] = jnp.sum(total, axis=0, keepdims=True)


def convolve(heads, rel_rows, ent_ref, band_ref, bias_ref, fcb_ref, fc_ref, pre2_out, slopes, picture, work, ready):
    table = ent_ref[...].astype(bf16)
    picture[:D, :] = dot(table, hits(heads, table.shape[1]))
    picture[D:, :] = rel_rows
    pre2 = jnp.zeros(pre2_out.shape, f32)
    for pair in range(PAIRS):
        first = pair * 2 * EMB_W
        window = jnp.transpose(picture[first : first + WINDOW, :]).astype(bf16)
        pre1 = dot(window, band_ref[...]) + bias_ref[...]
        sigma = sigmoid(pre1)
        act = pre1 * sigma
        slopes[pair] = sigma + act * (1.0 - sigma)
        work[pair] = act.astype(bf16)
        ready(pair)
        pre2 = pre2 + dot(work[pair], fc_ref[pair])
    pre2_out[...] = pre2 + fcb_ref[...]


def first_kernel(
    fc_hbm, taps_ref, heads_ref, ent_ref, rel_ref, bias_ref, fcb_ref,
    pre2_out, slopes, fc_out, band_out, band_t_out,
    picture, work, left, right, fc_ref, sems,
):
    prepare(fc_hbm, taps_ref, band_out, band_t_out, fc_ref, sems, left, right)

    def ready(pair):
        regroup(pair, fc_out, left, right)

    convolve(
        heads_ref[0:1, :], rel_ref[...], ent_ref, band_out, bias_ref, fcb_ref, fc_out,
        pre2_out, slopes, picture, work, ready,
    )


def forward_kernel(
    round_index, fc_ref, heads_ref, ent_ref, own_ref, other_ref, rows_ref, state_ref, band_ref, bias_ref, fcb_ref,
    pre2_out, slopes, _, picture, work,
):
    gradient = (own_ref[...] + other_ref[...])[:D, :]
    state = state_ref[...] + jnp.mean(gradient * gradient, axis=0, keepdims=True)
    rel_rows = rows_ref[...] - gradient * (learn_rate * lax.rsqrt(state))
    rel_rows = rel_rows.astype(bf16).astype(f32)
    convolve(
        heads_ref[round_index : round_index + 1, :], rel_rows, ent_ref, band_ref, bias_ref, fcb_ref, fc_ref,
        pre2_out, slopes, picture, work, lambda pair: None,
    )


def score_kernel(pre2_ref, tail_ref, neg_ref, grad_out, tail_out, neg_out):
    pre2 = pre2_ref[...]
    sigma = sigmoid(pre2)
    value = pre2 * sigma
    slope = sigma + value * (1.0 - sigma)
    query = value.astype(bf16)
    query32 = query.astype(f32)
    tails = tail_ref[...].astype(f32)
    pos_grad = -sigmoid(-jnp.sum(query32 * tails, axis=1, keepdims=True))
    negset = neg_ref[...]
    neg_grad = (negative_weight * sigmoid(dot_nt(query, negset))).astype(bf16)
    query_grad = pos_grad * tails + dot(neg_grad, negset)
    grad_out[...] = (query_grad * slope).astype(bf16)
    tail_out[...] = pos_grad * query32
    neg_out[...] = dot_tn(neg_grad, query)


def backward_kernel(
    round_index, fc_ref, relations_ref, grad_ref, slopes, band_t_ref, pack_out, head_out, _, work, total
):
    pre2_grad = grad_ref[...]
    total[...] = jnp.zeros_like(total)
    for pair in range(PAIRS):
        act_grad = dot_nt(pre2_grad, fc_ref[pair])
        work[pair] = (act_grad * slopes[pair]).astype(bf16)
        part = dot(work[pair], band_t_ref[...])
        at = slice(pair * 2 * EMB_W, pair * 2 * EMB_W + WINDOW)
        total[at, :] = total[at, :] + jnp.transpose(part)[:WINDOW, :]
    head_out[...] = total[:D, :]
    relations = relations_ref[round_index : round_index + 1, :]
    high = relations >> 6
    low = relations - (high << 6)
    spare = lax.broadcasted_iota(i32, (PACK - D, LANES), 0)
    codes = jnp.where(spare == 0, high, jnp.where(spare == 1, low, 0)).astype(f32)
    pack_out[...] = jnp.concatenate([total[D:, :], codes], axis=0).astype(bf16)


def entity_kernel(
    round_index, negatives, heads_ref, asked_ref, next_ref, ent_ref, state_ref, head_ref, back_ref, other_ref, *outs
):
    count = ent_ref.shape[1]
    number = back_ref.shape[0] - negatives
    back = jnp.concatenate([back_ref[:number, :], back_ref[number:, :] + other_ref[...]], axis=0)
    grads = jnp.concatenate([head_ref[...], turned(back)], axis=1)
    high, low = halves(grads)
    named = jnp.concatenate(
        [heads_ref[round_index : round_index + 1, :], asked_ref[0:1, :], asked_ref[1:2, :]], axis=1
    )
    both = dot_nt(jnp.concatenate([high, low], axis=0), hits(named, count))
    gradient = both[:D, :] + both[D:, :]
    state = state_ref[...] + jnp.mean(gradient * gradient, axis=0, keepdims=True)
    rows = ent_ref[...] - gradient * (learn_rate * lax.rsqrt(state))
    outs[0][...] = rows
    outs[1][...] = state
    if len(outs) > 2:
        pick_answer(rows.astype(bf16), next_ref, negatives, outs[2])


def lay_packs(place_ref, groups, grads, names):
    index = 0
    for group in groups:
        for inner in range(group.shape[0]):
            at = slice(index * LANES, (index + 1) * LANES)
            block = group[place_ref[inner]]
            grads[:, at] = block
            codes = block[PACK - 16 :, :].astype(f32)[D - PACK + 16 :, :]
            names[0:1, at] = (codes[0:1, :] * 64.0 + codes[1:2, :]).astype(i32)
            index += 1


def need_kernel(round_index, place_ref, *refs):
    groups, (ids_ref, others_ref, own_out, send_out, grads, names) = refs[:4], refs[4:]
    lay_packs(place_ref, groups, grads, names)
    wide = names.shape[1]
    for ids, out in ((others_ref, send_out), (ids_ref, own_out)):
        column = as_column(ids[round_index : round_index + 1, :])
        hit = jnp.concatenate(
            [
                jnp.where(
                    column == names[0:1, at : at + LANES].astype(f32), 1.0, 0.0
                ).astype(bf16)
                for at in range(0, wide, LANES)
            ],
            axis=1,
        )
        out[...] = jnp.transpose(dot_nt(hit, grads[...]))


def sums_kernel(kinds, place_ref, *refs):
    packs, before, refs = refs[: kinds[0]], refs[kinds[0] : sum(kinds)], refs[sum(kinds) :]
    outs, grads, names = refs[:-2], refs[-2], refs[-1]
    lay_packs(place_ref, packs, grads, names)
    size = names.shape[1] // len(packs)
    for first in range(0, outs[0].shape[1], LANES):
        at = slice(first, first + LANES)
        hit = hits(names[0:1, :], LANES, first)
        parts = [
            dot_nt(grads[:, k * size : (k + 1) * size], hit[:, k * size : (k + 1) * size])[:D, :]
            for k in range(len(packs))
        ]
        if len(packs) == 4:
            outs[0][:, at] = (parts[0] + parts[1]) + (parts[2] + parts[3])
        elif len(packs) == 3:
            outs[0][:, at] = parts[0] + parts[1]
            outs[1][:, at] = parts[2]
        else:
            outs[0][:, at] = before[0][:, at] + (before[1][:, at] + parts[0])


def relation_kernel(rel_ref, state_ref, *refs):
    rows = rel_ref[...]
    state = state_ref[...]
    count = rows.shape[1]
    for index in range(ROUNDS):
        gradient = refs[2 * index][:, :count] + refs[2 * index + 1][:, :count]
        state = state + jnp.mean(gradient * gradient, axis=0, keepdims=True)
        rows = rows - gradient * (learn_rate * lax.rsqrt(state))
    refs[2 * ROUNDS][...] = rows
    refs[2 * ROUNDS + 1][...] = state


class Plan:
    def __init__(self, groups, shards):
        self.total = groups * shards
        self.shards = shards
        self.near = [1 << bit for bit in range(1, shards.bit_length() - 1)]
        self.far = [shards << bit for bit in range(groups.bit_length() - 1)]
        self.lead = self.near[::-1] + self.far[:-2]

    def route(self, mask):
        return [(at, at ^ mask) for at in range(self.total)]

    def partner(self, bit):
        return self.shards << bit

    def send(self, block, mask):
        return lax.ppermute(block, BOTH, self.route(mask))

    def places(self, me):
        mine = sum(((me & mask) != 0).astype(i32) << step for step, mask in enumerate(self.lead))
        return jnp.arange(1 << len(self.lead), dtype=i32) ^ mine


def together(*values):
    return lax.optimization_barrier(values)


def shards(
    plan,
    entity_rows,
    entity_state,
    relation_rows,
    relation_state,
    conv_weight,
    conv_bias,
    fc_weight,
    fc_bias,
    head_ids,
    rel_ids,
    tail_ids,
    neg_ids,
):
    number = head_ids.shape[1]
    negatives = neg_ids.shape[1]
    count = relation_rows.shape[0]
    wide = count + -count % LANES
    features = fc_weight.shape[0]
    group = 1 << len(plan.lead)
    send = plan.send
    me = lax.axis_index("group") * plan.shards + lax.axis_index("shard")
    place = plan.places(me)
    ent = entity_rows.T
    ent_state = entity_state[None, :]
    rel = relation_rows.T
    rel_state = relation_state[None, :]
    bias2 = fc_bias[None, :]
    next_door, beyond = plan.near[-1], plan.near[:-1]

    def asked_rows(answer, bit):
        near = send(answer, plan.partner(bit))
        side = send(answer[number:], plan.partner(bit) | next_door)
        return near, side

    wanted = call(
        wanted_kernel,
        "wanted",
        1,
        [shaped((2, LANES), i32)] * ROUNDS,
        (tail_ids, neg_ids),
        [pltpu.VMEM(tail_ids.shape, i32), pltpu.VMEM(neg_ids.shape, i32), pltpu.SemaphoreType.DMA((2,))],
        far=(0, 1),
    )
    requested = [send(wanted[0], plan.partner(0))]
    rel_first, rel_later, state_later = call(
        rows_kernel,
        "relation_rows",
        1,
        [shaped((D, number)), shaped((D, number)), shaped((1, number))],
        (rel_ids, rel, rel_state),
        [pltpu.VMEM((D, wide), f32)],
    )
    requested[0], rel_first, rel_later, state_later = together(
        requested[0], rel_first, rel_later, state_later
    )
    answer_shape = shaped((number + negatives, D), bf16)
    (answer,) = call(
        functools.partial(answer_kernel, negatives), "answer", 1, [answer_shape], (requested[0], ent)
    )
    near, side = asked_rows(answer, 0)
    taps = jnp.tile(conv_weight.reshape(FILTERS, 9).T.astype(f32), (1, WIDE // FILTERS))
    bias = jnp.tile(conv_bias[None, :], (1, WIDE // FILTERS))
    pre2, slopes, fc, band, band_t = call(
        first_kernel,
        "first_forward",
        6,
        [
            shaped((number, D)),
            shaped((PAIRS, number, WIDE)),
            shaped((PAIRS, WIDE, D), bf16),
            shaped((WINDOW, WIDE), bf16),
            shaped((WIDE, LANES), bf16),
        ],
        (fc_weight.T, taps, head_ids, ent, rel_first, bias, bias2),
        [
            pltpu.VMEM((PIXELS, number), f32),
            pltpu.VMEM((PAIRS, number, WIDE), bf16),
            pltpu.VMEM((features, LANES), f32),
            pltpu.VMEM((features, LANES), f32),
            pltpu.VMEM((D, features), bf16),
            pltpu.SemaphoreType.DMA((PAIRS,)),
        ],
        limit=LIMP,
        far=(0,),
        near_out=(1, 2),
    )
    near, side, band = together(near, side, band)
    negset = jnp.concatenate([near[number:], side], axis=0)
    for mask in beyond:
        negset = jnp.concatenate([negset, send(negset, mask)], axis=0)
    requested.append(send(wanted[1], plan.partner(1)))
    near, negset = together(near, negset)
    rel_others = send(rel_ids, 1)
    negset = jnp.concatenate([negset, send(negset, 1)], axis=0)

    def lay(sources):
        return [pltpu.VMEM((PACK, sources * LANES), bf16), pltpu.VMEM((8, sources * LANES), i32)]

    sums = []
    for r in range(ROUNDS):
        last = r == ROUNDS - 1
        if r > 0:
            pre2, slopes, fc = call(
                functools.partial(forward_kernel, r),
                "forward",
                2.5,
                [shaped((number, D)), shaped((PAIRS, number, WIDE)), shaped(fc.shape, bf16)],
                (fc, head_ids, ent, *rel_inputs, band, bias, bias2),
                [pltpu.VMEM((PIXELS, number), f32), pltpu.VMEM((PAIRS, number, WIDE), bf16)],
                limit=LIM,
                near=(0,),
                near_out=(1, 2),
                alias={0: 2},
            )
        grad2, tail_grad, neg_part = call(
            score_kernel,
            "scores",
            1,
            [shaped((number, D), bf16), shaped((number, D)), shaped((negset.shape[0], D))],
            (pre2, near[:number], negset),
        )
        if r == 0:
            grad2, neg_part, requested[1], rel_others = together(
                grad2, neg_part, requested[1], rel_others
            )
        half = neg_part.shape[0] // 2
        arrived = send(neg_part[half:], 1)
        pack, head_grad, fc = call(
            functools.partial(backward_kernel, r),
            "backward",
            3,
            [shaped((PACK, number), bf16), shaped((D, number)), shaped(fc.shape, bf16)],
            (fc, rel_ids, grad2, slopes, band_t),
            [
                pltpu.VMEM((PAIRS, number, WIDE), bf16),
                pltpu.VMEM((PIXELS, number), f32),
            ],
            limit=LIM,
            near=(0, 3),
            near_out=(2,),
            alias={0: 2},
        )
        pack, arrived = together(pack, arrived)
        share = neg_part[:half] + arrived
        packs = pack[None]
        lead = list(plan.lead)
        back = list(reversed(beyond))
        for step, mask in enumerate(lead):
            came = send(packs, mask)
            if step < len(back):
                half = share.shape[0] // 2
                arrived = send(share[half:], back[step])
                came, arrived = together(came, arrived)
                share = share[:half] + arrived
            elif step == len(lead) - 1:
                own_back = jnp.concatenate([tail_grad, share[:negatives]], axis=0)
                to_owner = send(own_back, plan.partner(r))
                to_side = send(share[negatives:], plan.partner(r) | next_door)
                came, to_owner, to_side = together(came, to_owner, to_side)
            packs = jnp.concatenate([packs, came], axis=0)
        one, other = plan.far[-2:]
        across = send(packs, one)
        along = send(packs, other)
        if last:
            (part,) = call(
                functools.partial(sums_kernel, (4, 0)),
                "relation_sums",
                3,
                [shaped((D, wide))],
                (place, *groups),
                lay(4 * group),
                scalars=1,
            )
            across, along, part, to_owner, to_side = together(across, along, part, to_owner, to_side)
            sums = [part, send(part, 1)]
        out_shape = [shaped(ent.shape), shaped(ent_state.shape)]
        outs = call(
            functools.partial(entity_kernel, r, negatives),
            "entity_update",
            1.5,
            out_shape if last else out_shape + [answer_shape],
            (
                head_ids,
                requested[r],
                requested[min(r + 1, ROUNDS - 1)],
                ent,
                ent_state,
                head_grad,
                to_owner,
                to_side,
            ),
        )
        ent, ent_state = outs[:2]
        if last:
            corner = send(across, other)
            early = call(
                functools.partial(sums_kernel, (3, 0)),
                "early_sums",
                3,
                [shaped((D, wide))] * 2,
                (place, packs, across, along),
                lay(3 * group),
                scalars=1,
            )
            corner, ent, ent_state, *rest = together(corner, ent, ent_state, *early, *sums)
            early, sums = rest[:2], rest[2:]
            (part,) = call(
                functools.partial(sums_kernel, (1, 2)),
                "late_sums",
                1,
                [shaped((D, wide))],
                (place, corner, *early),
                lay(group),
                scalars=1,
            )
            sums += [part, send(part, 1)]
        else:
            near, side = asked_rows(outs[2], r + 1)
            corner = send(across, other)
            groups = (packs, across, along, corner)
            near, side = together(near, side)
            negset = jnp.concatenate([near[number:], side], axis=0)
            for mask in beyond:
                negset = jnp.concatenate([negset, send(negset, mask)], axis=0)
            own, partial = call(
                functools.partial(need_kernel, r + 1),
                "need",
                1.5,
                [shaped((PACK, number))] * 2,
                (place, *groups, rel_ids, rel_others),
                lay(4 * group),
                scalars=1,
            )
            negset, own, partial = together(negset, own, partial)
            rel_inputs = (own, send(partial, 1), rel_later, state_later)
            negset = jnp.concatenate([negset, send(negset, 1)], axis=0)
    rel, rel_state = call(
        relation_kernel, "relation_update", 2, [shaped((D, count)), shaped((1, count))], (rel, rel_state, *sums)
    )
    return (ent.T, ent_state.reshape(-1), rel.T, rel_state.reshape(-1))


def solution(mesh):
    plan = Plan(mesh.shape["group"], mesh.shape["shard"])
    in_specs = (
        P(BOTH, None),
        P(BOTH),
        P(),
        P(),
        P(),
        P(),
        P(),
        P(),
        P(None, BOTH),
        P(None, BOTH),
        P(None, BOTH),
        P(None, BOTH),
    )
    out_specs = (P(BOTH, None), P(BOTH), P(), P())
    return jax.shard_map(
        functools.partial(shards, plan),
        mesh=mesh,
        in_specs=in_specs,
        out_specs=out_specs,
        check_vma=False,
    )
```

```python
import functools

import jax
import jax.numpy as jnp
from jax import lax
from jax.experimental import pallas as pl
from jax.experimental.pallas import tpu as pltpu
from jax.sharding import PartitionSpec as P

EMB_W = 20
D = 200
FILTERS = 32
PIXELS = 400
SIDE = 18
PAIRS = 9
WINDOW = 80
WIDE = 1152
PACK = 208
LANES = 128
ROUNDS = 2
LIM = 24
LIMP = 28

negative_weight = 0.03125
learn_rate = 0.5

f32 = jnp.float32
bf16 = jnp.bfloat16
i32 = jnp.int32
BOTH = ("group", "shard")
VMEM = pl.BlockSpec(memory_space=pltpu.VMEM)
SMEM = pl.BlockSpec(memory_space=pltpu.SMEM)
HBM = pl.BlockSpec(memory_space=pltpu.HBM)


def shaped(shape, dtype=f32):
    return jax.ShapeDtypeStruct(shape, dtype)


def call(kernel, name, micros, out_shape, args, scratch=(), scalars=0, limit=16, far=(), near=(), near_out=(), alias=None):
    places = [SMEM] * scalars + [VMEM] * (len(args) - scalars)
    args = [
        pltpu.with_memory_space_constraint(arg, pltpu.HBM)
        if index in far
        else pltpu.with_memory_space_constraint(arg, pltpu.VMEM)
        if index in near
        else arg
        for index, arg in enumerate(args)
    ]
    return pl.pallas_call(
        kernel,
        out_shape=[
            pltpu.VMEM(out.shape, out.dtype) if index in near_out else out
            for index, out in enumerate(out_shape)
        ],
        input_output_aliases=alias or {},
        in_specs=[HBM if index in far else spec for index, spec in enumerate(places)],
        out_specs=[VMEM] * len(out_shape),
        scratch_shapes=list(scratch),
        compiler_params=pltpu.CompilerParams(vmem_limit_bytes=limit * 1024 * 1024),
        cost_estimate=pl.CostEstimate(
            flops=int(micros * 3e9), bytes_accessed=int(micros * 9e6), transcendentals=0
        ),
        name=name,
    )(*args)


def sigmoid(values):
    return 0.5 * jnp.tanh(0.5 * values) + 0.5


def dot(left, right):
    return jnp.dot(left, right, preferred_element_type=f32)


def dot_nt(left, right):
    return lax.dot_general(left, right, (((1,), (1,)), ((), ())), preferred_element_type=f32)


def dot_tn(left, right):
    return lax.dot_general(left, right, (((0,), (0,)), ((), ())), preferred_element_type=f32)


def as_column(row):
    return jnp.transpose(jnp.broadcast_to(row.astype(f32), (LANES, LANES)))


def hits(names_row, count, first=0):
    spot = lax.broadcasted_iota(i32, (count, names_row.shape[1]), 0) + first
    return jnp.where(spot == names_row, 1.0, 0.0).astype(bf16)


def halves(values):
    high = values.astype(bf16)
    return high, (values - high.astype(f32)).astype(bf16)


def padded(values, lanes):
    rest = lanes - values.shape[1]
    return jnp.concatenate([values, jnp.zeros((values.shape[0], rest), values.dtype)], axis=1)


def turned(values):
    rest = -values.shape[0] % LANES
    return jnp.transpose(jnp.concatenate([values, jnp.zeros((rest, D), f32)], axis=0))


def wanted_kernel(tails_hbm, negatives_hbm, *refs):
    outs, (tails_ref, negatives_ref, sems) = refs[:ROUNDS], refs[ROUNDS:]
    copies = [
        pltpu.make_async_copy(tails_hbm, tails_ref, sems.at[0]),
        pltpu.make_async_copy(negatives_hbm, negatives_ref, sems.at[1]),
    ]
    for copy in copies:
        copy.start()
    for copy in copies:
        copy.wait()
    for index, out in enumerate(outs):
        out[0:1, :] = tails_ref[index : index + 1, :]
        out[1:2, :] = padded(negatives_ref[index : index + 1, :], LANES)


def pick_answer(table, ids_ref, negatives, out):
    count = table.shape[1]
    number = out.shape[0] - negatives
    tails = dot(table, hits(ids_ref[0:1, :], count))
    out[:number, :] = jnp.transpose(tails).astype(bf16)
    negs = dot(table, hits(ids_ref[1:2, :], count))
    out[number:, :] = jnp.transpose(negs)[:negatives, :].astype(bf16)


def answer_kernel(negatives, ids_ref, ent_ref, out):
    pick_answer(ent_ref[...].astype(bf16), ids_ref, negatives, out)


def prepare(fc_hbm, taps_ref, band_out, band_t_out, fc_ref, sems, left, right):
    copies = []
    for pair in range(PAIRS):
        at = pl.ds(pair * WIDE, WIDE)
        copies.append(pltpu.make_async_copy(fc_hbm.at[:, at], fc_ref.at[:, at], sems.at[pair]))
        copies[-1].start()
    group = lax.broadcasted_iota(i32, (WINDOW, WIDE), 1) >> 5
    start = group + jnp.where(group >= SIDE, EMB_W - SIDE, 0)
    gap = lax.broadcasted_iota(i32, (WINDOW, WIDE), 0) - start
    band = jnp.zeros((WINDOW, WIDE), f32)
    for row_off in range(3):
        for col_off in range(3):
            tap = row_off * 3 + col_off
            hit = gap == EMB_W * row_off + col_off
            band = jnp.where(hit, taps_ref[tap : tap + 1, :], band)
    band_out[...] = band.astype(bf16)
    band_t_out[...] = jnp.transpose(
        jnp.concatenate([band, jnp.zeros((LANES - WINDOW, WIDE), f32)], axis=0)
    ).astype(bf16)
    for copy in copies:
        copy.wait()
    blank = jnp.zeros((2 * LANES - D, LANES), f32)
    for index in range(fc_ref.shape[1] // LANES):
        at = slice(index * LANES, (index + 1) * LANES)
        block = fc_ref[:, at].astype(f32)
        left[at, :] = jnp.transpose(block[:LANES])
        right[at, :] = jnp.transpose(jnp.concatenate([block[LANES:], blank], axis=0))


def regroup(pair, fc_out, left, right):
    spots = SIDE * SIDE
    each = spots // PAIRS
    for index in range(each):
        low = left[pl.ds(pair * each + index, FILTERS, stride=spots), :]
        high = right[pl.ds(pair * each + index, FILTERS, stride=spots), :]
        at = slice(index * FILTERS, (index + 1) * FILTERS)
        fc_out[pair, at, :LANES] = low.astype(bf16)
        fc_out[pair, at, LANES:] = high[:, : D - LANES].astype(bf16)


def rows_kernel(ids_ref, rel_ref, state_ref, first_out, later_out, state_out, table):
    count = rel_ref.shape[1]
    whole = count // LANES * LANES
    table[:, :whole] = rel_ref[:, :whole]
    rest = jnp.concatenate(
        [rel_ref[:, whole:], jnp.zeros((D, LANES - count + whole), f32)], axis=1
    )
    table[:, whole:] = rest
    values = table[...]
    wide = values.shape[1]
    high = values.astype(bf16)
    first_out[...] = dot(high, hits(ids_ref[0:1, :], wide))
    left = values - high.astype(f32)
    middle = left.astype(bf16)
    low = (left - middle.astype(f32)).astype(bf16)
    hit = hits(ids_ref[1:2, :], wide)
    later_out[...] = dot(high, hit) + dot(middle, hit) + dot(low, hit)
    sums = padded(state_ref[...], wide)
    names = ids_ref[1:2, :]
    total = jnp.zeros((LANES, LANES), f32)
    for block in range(wide // LANES):
        states = as_column(sums[:, block * LANES : (block + 1) * LANES])
        spot = lax.broadcasted_iota(i32, (LANES, LANES), 0) + block * LANES
        total = total + jnp.where(spot == names, states, 0.0)
    state_out[...] = jnp.sum(total, axis=0, keepdims=True)


def convolve(heads, rel_rows, ent_ref, band_ref, bias_ref, fcb_ref, fc_ref, pre2_out, slopes, picture, work, ready):
    table = ent_ref[...].astype(bf16)
    picture[:D, :] = dot(table, hits(heads, table.shape[1]))
    picture[D:, :] = rel_rows
    pre2 = jnp.zeros(pre2_out.shape, f32)
    for pair in range(PAIRS):
        first = pair * 2 * EMB_W
        window = jnp.transpose(picture[first : first + WINDOW, :]).astype(bf16)
        pre1 = dot(window, band_ref[...]) + bias_ref[...]
        sigma = sigmoid(pre1)
        act = pre1 * sigma
        slopes[pair] = sigma + act * (1.0 - sigma)
        work[pair] = act.astype(bf16)
        ready(pair)
        pre2 = pre2 + dot(work[pair], fc_ref[pair])
    pre2_out[...] = pre2 + fcb_ref[...]


def first_kernel(
    fc_hbm, taps_ref, heads_ref, ent_ref, rel_ref, bias_ref, fcb_ref,
    pre2_out, slopes, fc_out, band_out, band_t_out,
    picture, work, left, right, fc_ref, sems,
):
    prepare(fc_hbm, taps_ref, band_out, band_t_out, fc_ref, sems, left, right)

    def ready(pair):
        regroup(pair, fc_out, left, right)

    convolve(
        heads_ref[0:1, :], rel_ref[...], ent_ref, band_out, bias_ref, fcb_ref, fc_out,
        pre2_out, slopes, picture, work, ready,
    )


def forward_kernel(
    round_index, fc_ref, heads_ref, ent_ref, own_ref, other_ref, rows_ref, state_ref, band_ref, bias_ref, fcb_ref,
    pre2_out, slopes, fc_same, ent_same, picture, work,
):
    gradient = (own_ref[...] + other_ref[...])[:D, :]
    state = state_ref[...] + jnp.mean(gradient * gradient, axis=0, keepdims=True)
    rel_rows = rows_ref[...] - gradient * (learn_rate * lax.rsqrt(state))
    rel_rows = rel_rows.astype(bf16).astype(f32)
    convolve(
        heads_ref[round_index : round_index + 1, :], rel_rows, ent_ref, band_ref, bias_ref, fcb_ref, fc_ref,
        pre2_out, slopes, picture, work, lambda pair: None,
    )


def score_kernel(pre2_ref, tail_ref, neg_ref, grad_out, tail_out, neg_out):
    pre2 = pre2_ref[...]
    sigma = sigmoid(pre2)
    value = pre2 * sigma
    slope = sigma + value * (1.0 - sigma)
    query = value.astype(bf16)
    query32 = query.astype(f32)
    tails = tail_ref[...].astype(f32)
    pos_grad = -sigmoid(-jnp.sum(query32 * tails, axis=1, keepdims=True))
    negset = neg_ref[...]
    neg_grad = (negative_weight * sigmoid(dot_nt(query, negset))).astype(bf16)
    query_grad = pos_grad * tails + dot(neg_grad, negset)
    grad_out[...] = (query_grad * slope).astype(bf16)
    tail_out[...] = pos_grad * query32
    neg_out[...] = dot_tn(neg_grad, query)


def backward_kernel(
    round_index, fc_ref, relations_ref, grad_ref, slopes, band_t_ref, pack_out, head_out, _, work, total
):
    pre2_grad = grad_ref[...]
    total[...] = jnp.zeros_like(total)
    for pair in range(PAIRS):
        act_grad = dot_nt(pre2_grad, fc_ref[pair])
        work[pair] = (act_grad * slopes[pair]).astype(bf16)
        part = dot(work[pair], band_t_ref[...])
        at = slice(pair * 2 * EMB_W, pair * 2 * EMB_W + WINDOW)
        total[at, :] = total[at, :] + jnp.transpose(part)[:WINDOW, :]
    head_out[...] = total[:D, :]
    relations = relations_ref[round_index : round_index + 1, :]
    high = relations >> 6
    low = relations - (high << 6)
    spare = lax.broadcasted_iota(i32, (PACK - D, LANES), 0)
    codes = jnp.where(spare == 0, high, jnp.where(spare == 1, low, 0)).astype(f32)
    pack_out[...] = jnp.concatenate([total[D:, :], codes], axis=0).astype(bf16)


def entity_kernel(
    round_index, negatives, heads_ref, asked_ref, next_ref, ent_ref, state_ref, head_ref, back_ref, other_ref, *outs
):
    count = ent_ref.shape[1]
    number = back_ref.shape[0] - negatives
    back = back_ref[...].astype(f32)
    back = jnp.concatenate([back[:number, :], back[number:, :] + other_ref[...].astype(f32)], axis=0)
    grads = jnp.concatenate([head_ref[...], turned(back)], axis=1)
    high, low = halves(grads)
    named = jnp.concatenate(
        [heads_ref[round_index : round_index + 1, :], asked_ref[0:1, :], asked_ref[1:2, :]], axis=1
    )
    both = dot_nt(jnp.concatenate([high, low], axis=0), hits(named, count))
    gradient = both[:D, :] + both[D:, :]
    state = state_ref[...] + jnp.mean(gradient * gradient, axis=0, keepdims=True)
    rows = ent_ref[...] - gradient * (learn_rate * lax.rsqrt(state))
    outs[0][...] = rows
    outs[1][...] = state
    if len(outs) > 2:
        pick_answer(rows.astype(bf16), next_ref, negatives, outs[2])


def lay_packs(place_ref, groups, grads, names):
    index = 0
    for group in groups:
        for inner in range(group.shape[0]):
            at = slice(index * LANES, (index + 1) * LANES)
            block = group[place_ref[inner]]
            grads[:, at] = block
            codes = block[PACK - 16 :, :].astype(f32)[D - PACK + 16 :, :]
            names[0:1, at] = (codes[0:1, :] * 64.0 + codes[1:2, :]).astype(i32)
            index += 1


def need_kernel(round_index, place_ref, *refs):
    groups, (ids_ref, others_ref, own_out, send_out, grads, names) = refs[:4], refs[4:]
    lay_packs(place_ref, groups, grads, names)
    wide = names.shape[1]
    for ids, out in ((others_ref, send_out), (ids_ref, own_out)):
        column = as_column(ids[round_index : round_index + 1, :])
        hit = jnp.concatenate(
            [
                jnp.where(
                    column == names[0:1, at : at + LANES].astype(f32), 1.0, 0.0
                ).astype(bf16)
                for at in range(0, wide, LANES)
            ],
            axis=1,
        )
        out[...] = jnp.transpose(dot_nt(hit, grads[...]))


def sums_kernel(kinds, place_ref, *refs):
    packs, before, refs = refs[: kinds[0]], refs[kinds[0] : sum(kinds)], refs[sum(kinds) :]
    outs, grads, names = refs[:-2], refs[-2], refs[-1]
    lay_packs(place_ref, packs, grads, names)
    size = names.shape[1] // len(packs)
    for first in range(0, outs[0].shape[1], LANES):
        at = slice(first, first + LANES)
        hit = hits(names[0:1, :], LANES, first)
        parts = [
            dot_nt(grads[:, k * size : (k + 1) * size], hit[:, k * size : (k + 1) * size])[:D, :]
            for k in range(len(packs))
        ]
        if len(packs) == 4:
            outs[0][:, at] = (parts[0] + parts[1]) + (parts[2] + parts[3])
        elif len(packs) == 3:
            outs[0][:, at] = parts[0] + parts[1]
            outs[1][:, at] = parts[2]
        else:
            outs[0][:, at] = before[0][:, at] + (before[1][:, at] + parts[0])


def relation_kernel(rel_ref, state_ref, *refs):
    rows = rel_ref[...]
    state = state_ref[...]
    count = rows.shape[1]
    for index in range(ROUNDS):
        gradient = refs[2 * index][:, :count] + refs[2 * index + 1][:, :count]
        state = state + jnp.mean(gradient * gradient, axis=0, keepdims=True)
        rows = rows - gradient * (learn_rate * lax.rsqrt(state))
    refs[2 * ROUNDS][...] = rows
    refs[2 * ROUNDS + 1][...] = state[0]


class Plan:
    def __init__(self, groups, shards):
        self.total = groups * shards
        self.shards = shards
        self.near = [1 << bit for bit in range(1, shards.bit_length() - 1)]
        self.far = [shards << bit for bit in range(groups.bit_length() - 1)]
        self.lead = self.near[::-1] + self.far[:-2]

    def route(self, mask):
        return [(at, at ^ mask) for at in range(self.total)]

    def partner(self, bit):
        return self.shards << bit

    def send(self, block, mask):
        return lax.ppermute(block, BOTH, self.route(mask))

    def places(self, me):
        mine = sum(((me & mask) != 0).astype(i32) << step for step, mask in enumerate(self.lead))
        return jnp.arange(1 << len(self.lead), dtype=i32) ^ mine


def together(*values):
    return lax.optimization_barrier(values)


def shards(
    plan,
    entity_rows,
    entity_state,
    relation_rows,
    relation_state,
    conv_weight,
    conv_bias,
    fc_weight,
    fc_bias,
    head_ids,
    rel_ids,
    tail_ids,
    neg_ids,
):
    number = head_ids.shape[1]
    negatives = neg_ids.shape[1]
    count = relation_rows.shape[0]
    wide = count + -count % LANES
    features = fc_weight.shape[0]
    group = 1 << len(plan.lead)
    send = plan.send
    me = lax.axis_index("group") * plan.shards + lax.axis_index("shard")
    place = plan.places(me)
    ent = entity_rows.T
    ent_state = entity_state[None, :]
    rel = relation_rows.T
    rel_state = relation_state[None, :]
    bias2 = fc_bias[None, :]
    next_door, beyond = plan.near[-1], plan.near[:-1]

    def asked_rows(answer, bit):
        near = send(answer, plan.partner(bit))
        side = send(answer[number:], plan.partner(bit) | next_door)
        return near, side

    wanted = call(
        wanted_kernel,
        "wanted",
        1,
        [shaped((2, LANES), i32)] * ROUNDS,
        (tail_ids, neg_ids),
        [pltpu.VMEM(tail_ids.shape, i32), pltpu.VMEM(neg_ids.shape, i32), pltpu.SemaphoreType.DMA((2,))],
        far=(0, 1),
    )
    requested = [send(wanted[0], plan.partner(0))]
    rel_first, rel_later, state_later = call(
        rows_kernel,
        "relation_rows",
        1,
        [shaped((D, number)), shaped((D, number)), shaped((1, number))],
        (rel_ids, rel, rel_state),
        [pltpu.VMEM((D, wide), f32)],
    )
    requested[0], rel_first, rel_later, state_later = together(
        requested[0], rel_first, rel_later, state_later
    )
    answer_shape = shaped((number + negatives, D), bf16)
    (answer,) = call(
        functools.partial(answer_kernel, negatives), "answer", 1, [answer_shape], (requested[0], ent)
    )
    near, side = asked_rows(answer, 0)
    taps = jnp.tile(conv_weight.reshape(FILTERS, 9).T.astype(f32), (1, WIDE // FILTERS))
    bias = jnp.tile(conv_bias[None, :], (1, WIDE // FILTERS))
    pre2, slopes, fc, band, band_t = call(
        first_kernel,
        "first_forward",
        6,
        [
            shaped((number, D)),
            shaped((PAIRS, number, WIDE)),
            shaped((PAIRS, WIDE, D), bf16),
            shaped((WINDOW, WIDE), bf16),
            shaped((WIDE, LANES), bf16),
        ],
        (fc_weight.T, taps, head_ids, ent, rel_first, bias, bias2),
        [
            pltpu.VMEM((PIXELS, number), f32),
            pltpu.VMEM((PAIRS, number, WIDE), bf16),
            pltpu.VMEM((features, LANES), f32),
            pltpu.VMEM((features, LANES), f32),
            pltpu.VMEM((D, features), bf16),
            pltpu.SemaphoreType.DMA((PAIRS,)),
        ],
        limit=LIMP,
        far=(0,),
        near_out=(1, 2),
    )
    near, side, band = together(near, side, band)
    negset = jnp.concatenate([near[number:], side], axis=0)
    for mask in beyond:
        negset = jnp.concatenate([negset, send(negset, mask)], axis=0)
    requested.append(send(wanted[1], plan.partner(1)))
    near, negset = together(near, negset)
    rel_others = send(rel_ids, 1)
    negset = jnp.concatenate([negset, send(negset, 1)], axis=0)

    def lay(sources):
        return [pltpu.VMEM((PACK, sources * LANES), bf16), pltpu.VMEM((8, sources * LANES), i32)]

    sums = []
    for r in range(ROUNDS):
        last = r == ROUNDS - 1
        if r > 0:
            pre2, slopes, fc, ent = call(
                functools.partial(forward_kernel, r),
                "forward",
                2.5,
                [
                    shaped((number, D)),
                    shaped((PAIRS, number, WIDE)),
                    shaped(fc.shape, bf16),
                    shaped(ent.shape),
                ],
                (fc, head_ids, ent, *rel_inputs, band, bias, bias2),
                [pltpu.VMEM((PIXELS, number), f32), pltpu.VMEM((PAIRS, number, WIDE), bf16)],
                limit=LIM,
                near=(0, 2),
                near_out=(1, 2, 3),
                alias={0: 2, 2: 3},
            )
        grad2, tail_grad, neg_part = call(
            score_kernel,
            "scores",
            1,
            [shaped((number, D), bf16), shaped((number, D)), shaped((negset.shape[0], D))],
            (pre2, near[:number], negset),
        )
        if r == 0:
            grad2, neg_part, rel_others = together(grad2, neg_part, rel_others)
        half = neg_part.shape[0] // 2
        arrived = send(neg_part[half:], 1)
        pack, head_grad, fc = call(
            functools.partial(backward_kernel, r),
            "backward",
            3,
            [shaped((PACK, number), bf16), shaped((D, number)), shaped(fc.shape, bf16)],
            (fc, rel_ids, grad2, slopes, band_t),
            [
                pltpu.VMEM((PAIRS, number, WIDE), bf16),
                pltpu.VMEM((PIXELS, number), f32),
            ],
            limit=LIM,
            near=(0, 3),
            near_out=(2,),
            alias={0: 2},
        )
        pack, arrived = together(pack, arrived)
        share = neg_part[:half] + arrived
        packs = pack[None]
        lead = list(plan.lead)
        if last:
            before = call(
                functools.partial(sums_kernel, (3, 0)),
                "early_sums",
                3,
                [shaped((D, wide))] * 2,
                (place, *groups[:3]),
                lay(3 * group),
                scalars=1,
            )
        back = list(reversed(beyond))
        for step, mask in enumerate(lead):
            came = send(packs, mask)
            if step < len(back):
                half = share.shape[0] // 2
                arrived = send(share[half:], back[step])
                if last:
                    came, arrived, *before = together(came, arrived, *before)
                    (part,) = call(
                        functools.partial(sums_kernel, (1, 2)),
                        "late_sums",
                        1,
                        [shaped((D, wide))],
                        (place, groups[3], *before),
                        lay(group),
                        scalars=1,
                    )
                else:
                    came, arrived, requested[1] = together(came, arrived, requested[1])
                share = share[:half] + arrived
            elif step == len(lead) - 1:
                own_back = jnp.concatenate([tail_grad, share[:negatives]], axis=0).astype(bf16)
                side_back = share[negatives:].astype(bf16)
                to_owner = send(own_back, plan.partner(r))
                to_side = send(side_back, plan.partner(r) | next_door)
                if last:
                    came, to_owner, to_side, part = together(came, to_owner, to_side, part)
            packs = jnp.concatenate([packs, came], axis=0)
        one, other = plan.far[-2:]
        across = send(packs, one)
        along = send(packs, other)
        out_shape = [shaped(ent.shape), shaped(ent_state.shape)]
        outs = call(
            functools.partial(entity_kernel, r, negatives),
            "entity_update",
            1.5,
            out_shape if last else out_shape + [answer_shape],
            (
                head_ids,
                requested[r],
                requested[min(r + 1, ROUNDS - 1)],
                ent,
                ent_state,
                head_grad,
                to_owner,
                to_side,
            ),
            near=(3,) if last else (),
            near_out=() if last else (0,),
        )
        ent, ent_state = outs[:2]
        if last:
            across, along, ent, ent_state, part = together(across, along, ent, ent_state, part)
            sums = [part, send(part, 1)]
            corner = send(across, other)
            early = call(
                functools.partial(sums_kernel, (3, 0)),
                "early_sums",
                3,
                [shaped((D, wide))] * 2,
                (place, packs, across, along),
                lay(3 * group),
                scalars=1,
            )
            corner, *early = together(corner, *early)
            (part,) = call(
                functools.partial(sums_kernel, (1, 2)),
                "late_sums",
                1,
                [shaped((D, wide))],
                (place, corner, *early),
                lay(group),
                scalars=1,
            )
            sums += [part, send(part, 1)]
        else:
            near, side = asked_rows(outs[2], r + 1)
            corner = send(across, other)
            groups = (packs, across, along, corner)
            near, side = together(near, side)
            negset = jnp.concatenate([near[number:], side], axis=0)
            for mask in beyond:
                negset = jnp.concatenate([negset, send(negset, mask)], axis=0)
            own, partial = call(
                functools.partial(need_kernel, r + 1),
                "need",
                1.5,
                [shaped((PACK, number))] * 2,
                (place, *groups, rel_ids, rel_others),
                lay(4 * group),
                scalars=1,
            )
            negset, own, partial = together(negset, own, partial)
            rel_inputs = (own, send(partial, 1), rel_later, state_later)
            negset = jnp.concatenate([negset, send(negset, 1)], axis=0)
    rel, rel_state = call(
        relation_kernel, "relation_update", 2, [shaped((D, count)), shaped((count,))], (rel, rel_state, *sums)
    )
    return (ent.T, ent_state.reshape(-1), rel.T, rel_state)


def solution(mesh):
    plan = Plan(mesh.shape["group"], mesh.shape["shard"])
    in_specs = (
        P(BOTH, None),
        P(BOTH),
        P(),
        P(),
        P(),
        P(),
        P(),
        P(),
        P(None, BOTH),
        P(None, BOTH),
        P(None, BOTH),
        P(None, BOTH),
    )
    out_specs = (P(BOTH, None), P(BOTH), P(), P())
    return jax.shard_map(
        functools.partial(shards, plan),
        mesh=mesh,
        in_specs=in_specs,
        out_specs=out_specs,
        check_vma=False,
    )
```

```python
import functools

import jax
import jax.numpy as jnp
from jax import lax
from jax.experimental import pallas as pl
from jax.experimental.pallas import tpu as pltpu
from jax.sharding import PartitionSpec as P

EMB_W = 20
D = 200
FILTERS = 32
PIXELS = 400
SIDE = 18
PAIRS = 9
WINDOW = 80
WIDE = 1152
PACK = 208
LANES = 128
ROUNDS = 2
LIM = 24
LIMP = 28

negative_weight = 0.03125
learn_rate = 0.5

f32 = jnp.float32
bf16 = jnp.bfloat16
i32 = jnp.int32
BOTH = ("group", "shard")
VMEM = pl.BlockSpec(memory_space=pltpu.VMEM)
SMEM = pl.BlockSpec(memory_space=pltpu.SMEM)
HBM = pl.BlockSpec(memory_space=pltpu.HBM)


def shaped(shape, dtype=f32):
    return jax.ShapeDtypeStruct(shape, dtype)


def call(kernel, name, micros, out_shape, args, scratch=(), scalars=0, limit=16, far=(), near=(), near_out=(), alias=None):
    places = [SMEM] * scalars + [VMEM] * (len(args) - scalars)
    args = [
        pltpu.with_memory_space_constraint(arg, pltpu.HBM)
        if index in far
        else pltpu.with_memory_space_constraint(arg, pltpu.VMEM)
        if index in near
        else arg
        for index, arg in enumerate(args)
    ]
    return pl.pallas_call(
        kernel,
        out_shape=[
            pltpu.VMEM(out.shape, out.dtype) if index in near_out else out
            for index, out in enumerate(out_shape)
        ],
        input_output_aliases=alias or {},
        in_specs=[HBM if index in far else spec for index, spec in enumerate(places)],
        out_specs=[VMEM] * len(out_shape),
        scratch_shapes=list(scratch),
        compiler_params=pltpu.CompilerParams(vmem_limit_bytes=limit * 1024 * 1024),
        cost_estimate=pl.CostEstimate(
            flops=int(micros * 3e9), bytes_accessed=int(micros * 9e6), transcendentals=0
        ),
        name=name,
    )(*args)


def sigmoid(values):
    return 0.5 * jnp.tanh(0.5 * values) + 0.5


def dot(left, right):
    return jnp.dot(left, right, preferred_element_type=f32)


def dot_nt(left, right):
    return lax.dot_general(left, right, (((1,), (1,)), ((), ())), preferred_element_type=f32)


def dot_tn(left, right):
    return lax.dot_general(left, right, (((0,), (0,)), ((), ())), preferred_element_type=f32)


def as_column(row):
    return jnp.transpose(jnp.broadcast_to(row.astype(f32), (LANES, LANES)))


def hits(names_row, count, first=0):
    spot = lax.broadcasted_iota(i32, (count, names_row.shape[1]), 0) + first
    return jnp.where(spot == names_row, 1.0, 0.0).astype(bf16)


def halves(values):
    high = values.astype(bf16)
    return high, (values - high.astype(f32)).astype(bf16)


def padded(values, lanes):
    rest = lanes - values.shape[1]
    return jnp.concatenate([values, jnp.zeros((values.shape[0], rest), values.dtype)], axis=1)


def turned(values):
    rest = -values.shape[0] % LANES
    return jnp.transpose(jnp.concatenate([values, jnp.zeros((rest, D), f32)], axis=0))


def wanted_kernel(tails_hbm, negatives_hbm, *refs):
    outs, (tails_ref, negatives_ref, sems) = refs[:ROUNDS], refs[ROUNDS:]
    copies = [
        pltpu.make_async_copy(tails_hbm, tails_ref, sems.at[0]),
        pltpu.make_async_copy(negatives_hbm, negatives_ref, sems.at[1]),
    ]
    for copy in copies:
        copy.start()
    for copy in copies:
        copy.wait()
    for index, out in enumerate(outs):
        out[0:1, :] = tails_ref[index : index + 1, :]
        out[1:2, :] = padded(negatives_ref[index : index + 1, :], LANES)


def pick_answer(table, ids_ref, negatives, out):
    count = table.shape[1]
    number = out.shape[0] - negatives
    tails = dot(table, hits(ids_ref[0:1, :], count))
    out[:number, :] = jnp.transpose(tails).astype(bf16)
    negs = dot(table, hits(ids_ref[1:2, :], count))
    out[number:, :] = jnp.transpose(negs)[:negatives, :].astype(bf16)


def answer_kernel(negatives, ids_ref, ent_ref, out):
    pick_answer(ent_ref[...].astype(bf16), ids_ref, negatives, out)


def prepare(fc_hbm, taps_ref, band_out, band_t_out, fc_ref, sems, left, right):
    copies = []
    for pair in range(PAIRS):
        at = pl.ds(pair * WIDE, WIDE)
        copies.append(pltpu.make_async_copy(fc_hbm.at[:, at], fc_ref.at[:, at], sems.at[pair]))
        copies[-1].start()
    group = lax.broadcasted_iota(i32, (WINDOW, WIDE), 1) >> 5
    start = group + jnp.where(group >= SIDE, EMB_W - SIDE, 0)
    gap = lax.broadcasted_iota(i32, (WINDOW, WIDE), 0) - start
    band = jnp.zeros((WINDOW, WIDE), f32)
    for row_off in range(3):
        for col_off in range(3):
            tap = row_off * 3 + col_off
            hit = gap == EMB_W * row_off + col_off
            band = jnp.where(hit, taps_ref[tap : tap + 1, :], band)
    band_out[...] = band.astype(bf16)
    band_t_out[...] = jnp.transpose(
        jnp.concatenate([band, jnp.zeros((LANES - WINDOW, WIDE), f32)], axis=0)
    ).astype(bf16)
    for copy in copies:
        copy.wait()
    blank = jnp.zeros((2 * LANES - D, LANES), f32)
    for index in range(fc_ref.shape[1] // LANES):
        at = slice(index * LANES, (index + 1) * LANES)
        block = fc_ref[:, at].astype(f32)
        left[at, :] = jnp.transpose(block[:LANES])
        right[at, :] = jnp.transpose(jnp.concatenate([block[LANES:], blank], axis=0))


def regroup(pair, fc_out, left, right):
    spots = SIDE * SIDE
    each = spots // PAIRS
    for index in range(each):
        low = left[pl.ds(pair * each + index, FILTERS, stride=spots), :]
        high = right[pl.ds(pair * each + index, FILTERS, stride=spots), :]
        at = slice(index * FILTERS, (index + 1) * FILTERS)
        fc_out[pair, at, :LANES] = low.astype(bf16)
        fc_out[pair, at, LANES:] = high[:, : D - LANES].astype(bf16)


def rows_kernel(ids_ref, rel_ref, state_ref, first_out, later_out, state_out, table):
    count = rel_ref.shape[1]
    whole = count // LANES * LANES
    table[:, :whole] = rel_ref[:, :whole]
    rest = jnp.concatenate(
        [rel_ref[:, whole:], jnp.zeros((D, LANES - count + whole), f32)], axis=1
    )
    table[:, whole:] = rest
    values = table[...]
    wide = values.shape[1]
    high = values.astype(bf16)
    first_out[...] = dot(high, hits(ids_ref[0:1, :], wide))
    left = values - high.astype(f32)
    middle = left.astype(bf16)
    low = (left - middle.astype(f32)).astype(bf16)
    hit = hits(ids_ref[1:2, :], wide)
    later_out[...] = dot(high, hit) + dot(middle, hit) + dot(low, hit)
    sums = padded(state_ref[...], wide)
    names = ids_ref[1:2, :]
    total = jnp.zeros((LANES, LANES), f32)
    for block in range(wide // LANES):
        states = as_column(sums[:, block * LANES : (block + 1) * LANES])
        spot = lax.broadcasted_iota(i32, (LANES, LANES), 0) + block * LANES
        total = total + jnp.where(spot == names, states, 0.0)
    state_out[...] = jnp.sum(total, axis=0, keepdims=True)


def convolve(heads, rel_rows, ent_ref, band_ref, bias_ref, fcb_ref, fc_ref, pre2_out, slopes, picture, work, ready):
    table = ent_ref[...].astype(bf16)
    picture[:D, :] = dot(table, hits(heads, table.shape[1]))
    picture[D:, :] = rel_rows
    pre2 = jnp.zeros(pre2_out.shape, f32)
    for pair in range(PAIRS):
        first = pair * 2 * EMB_W
        window = jnp.transpose(picture[first : first + WINDOW, :]).astype(bf16)
        pre1 = dot(window, band_ref[...]) + bias_ref[...]
        sigma = sigmoid(pre1)
        act = pre1 * sigma
        slopes[pair] = sigma + act * (1.0 - sigma)
        work[pair] = act.astype(bf16)
        ready(pair)
        pre2 = pre2 + dot(work[pair], fc_ref[pair])
    pre2_out[...] = pre2 + fcb_ref[...]


def first_kernel(
    fc_hbm, taps_ref, heads_ref, ent_ref, rel_ref, bias_ref, fcb_ref,
    pre2_out, slopes, fc_out, band_out, band_t_out,
    picture, work, left, right, fc_ref, sems,
):
    prepare(fc_hbm, taps_ref, band_out, band_t_out, fc_ref, sems, left, right)

    def ready(pair):
        regroup(pair, fc_out, left, right)

    convolve(
        heads_ref[0:1, :], rel_ref[...], ent_ref, band_out, bias_ref, fcb_ref, fc_out,
        pre2_out, slopes, picture, work, ready,
    )


def forward_kernel(
    round_index, fc_ref, heads_ref, ent_ref, own_ref, other_ref, rows_ref, state_ref, band_ref, bias_ref, fcb_ref,
    pre2_out, slopes, fc_same, ent_same, picture, work,
):
    gradient = (own_ref[...] + other_ref[...])[:D, :]
    state = state_ref[...] + jnp.mean(gradient * gradient, axis=0, keepdims=True)
    rel_rows = rows_ref[...] - gradient * (learn_rate * lax.rsqrt(state))
    rel_rows = rel_rows.astype(bf16).astype(f32)
    convolve(
        heads_ref[round_index : round_index + 1, :], rel_rows, ent_ref, band_ref, bias_ref, fcb_ref, fc_ref,
        pre2_out, slopes, picture, work, lambda pair: None,
    )


def score_kernel(pre2_ref, tail_ref, neg_ref, grad_out, tail_out, neg_out):
    pre2 = pre2_ref[...]
    sigma = sigmoid(pre2)
    value = pre2 * sigma
    slope = sigma + value * (1.0 - sigma)
    query = value.astype(bf16)
    query32 = query.astype(f32)
    tails = tail_ref[...].astype(f32)
    pos_grad = -sigmoid(-jnp.sum(query32 * tails, axis=1, keepdims=True))
    negset = neg_ref[...]
    neg_grad = (negative_weight * sigmoid(dot_nt(query, negset))).astype(bf16)
    query_grad = pos_grad * tails + dot(neg_grad, negset)
    grad_out[...] = (query_grad * slope).astype(bf16)
    tail_out[...] = pos_grad * query32
    neg_out[...] = dot_tn(neg_grad, query)


def backward_kernel(
    round_index, fc_ref, relations_ref, grad_ref, slopes, band_t_ref, pack_out, head_out, _, work, total
):
    pre2_grad = grad_ref[...]
    total[...] = jnp.zeros_like(total)
    for pair in range(PAIRS):
        act_grad = dot_nt(pre2_grad, fc_ref[pair])
        work[pair] = (act_grad * slopes[pair]).astype(bf16)
        part = dot(work[pair], band_t_ref[...])
        at = slice(pair * 2 * EMB_W, pair * 2 * EMB_W + WINDOW)
        total[at, :] = total[at, :] + jnp.transpose(part)[:WINDOW, :]
    head_out[...] = total[:D, :]
    relations = relations_ref[round_index : round_index + 1, :]
    high = relations >> 6
    low = relations - (high << 6)
    spare = lax.broadcasted_iota(i32, (PACK - D, LANES), 0)
    codes = jnp.where(spare == 0, high, jnp.where(spare == 1, low, 0)).astype(f32)
    pack_out[...] = jnp.concatenate([total[D:, :], codes], axis=0).astype(bf16)


def entity_kernel(
    round_index, negatives, heads_ref, asked_ref, next_ref, ent_ref, state_ref, head_ref, back_ref, other_ref, *outs
):
    count = ent_ref.shape[1]
    number = back_ref.shape[0] - negatives
    back = back_ref[...].astype(f32)
    back = jnp.concatenate([back[:number, :], back[number:, :] + other_ref[...].astype(f32)], axis=0)
    grads = jnp.concatenate([head_ref[...], turned(back)], axis=1)
    high, low = halves(grads)
    named = jnp.concatenate(
        [heads_ref[round_index : round_index + 1, :], asked_ref[0:1, :], asked_ref[1:2, :]], axis=1
    )
    both = dot_nt(jnp.concatenate([high, low], axis=0), hits(named, count))
    gradient = both[:D, :] + both[D:, :]
    state = state_ref[...] + jnp.mean(gradient * gradient, axis=0, keepdims=True)
    rows = ent_ref[...] - gradient * (learn_rate * lax.rsqrt(state))
    outs[0][...] = rows
    outs[1][...] = state
    if len(outs) > 2:
        pick_answer(rows.astype(bf16), next_ref, negatives, outs[2])


def lay_packs(place_ref, groups, grads, names):
    index = 0
    for group in groups:
        for inner in range(group.shape[0]):
            at = slice(index * LANES, (index + 1) * LANES)
            block = group[place_ref[inner]]
            grads[:, at] = block
            codes = block[PACK - 16 :, :].astype(f32)[D - PACK + 16 :, :]
            names[0:1, at] = (codes[0:1, :] * 64.0 + codes[1:2, :]).astype(i32)
            index += 1


def need_kernel(round_index, place_ref, *refs):
    groups, (ids_ref, others_ref, own_out, send_out, grads, names) = refs[:4], refs[4:]
    lay_packs(place_ref, groups, grads, names)
    wide = names.shape[1]
    for ids, out in ((others_ref, send_out), (ids_ref, own_out)):
        column = as_column(ids[round_index : round_index + 1, :])
        hit = jnp.concatenate(
            [
                jnp.where(
                    column == names[0:1, at : at + LANES].astype(f32), 1.0, 0.0
                ).astype(bf16)
                for at in range(0, wide, LANES)
            ],
            axis=1,
        )
        out[...] = jnp.transpose(dot_nt(hit, grads[...]))


def sums_kernel(kinds, place_ref, *refs):
    packs, before, refs = refs[: kinds[0]], refs[kinds[0] : sum(kinds)], refs[sum(kinds) :]
    outs, grads, names = refs[:-2], refs[-2], refs[-1]
    lay_packs(place_ref, packs, grads, names)
    size = names.shape[1] // len(packs)
    for first in range(0, outs[0].shape[1], LANES):
        at = slice(first, first + LANES)
        hit = hits(names[0:1, :], LANES, first)
        parts = [
            dot_nt(grads[:, k * size : (k + 1) * size], hit[:, k * size : (k + 1) * size])[:D, :]
            for k in range(len(packs))
        ]
        if len(packs) == 4:
            outs[0][:, at] = (parts[0] + parts[1]) + (parts[2] + parts[3])
        elif len(packs) == 3:
            outs[0][:, at] = parts[0] + parts[1]
            outs[1][:, at] = parts[2]
        else:
            outs[0][:, at] = before[0][:, at] + (before[1][:, at] + parts[0])


def relation_kernel(rel_ref, state_ref, *refs):
    rows = rel_ref[...]
    state = state_ref[...]
    count = rows.shape[1]
    for index in range(ROUNDS):
        gradient = refs[2 * index][:, :count] + refs[2 * index + 1][:, :count]
        state = state + jnp.mean(gradient * gradient, axis=0, keepdims=True)
        rows = rows - gradient * (learn_rate * lax.rsqrt(state))
    refs[2 * ROUNDS][...] = rows
    refs[2 * ROUNDS + 1][...] = state[0]


class Plan:
    def __init__(self, groups, shards):
        self.total = groups * shards
        self.shards = shards
        self.near = [1 << bit for bit in range(1, shards.bit_length() - 1)]
        self.far = [shards << bit for bit in range(groups.bit_length() - 1)]
        self.lead = self.near[::-1] + self.far[:-2]

    def route(self, mask):
        return [(at, at ^ mask) for at in range(self.total)]

    def partner(self, bit):
        return self.shards << bit

    def send(self, block, mask):
        return lax.ppermute(block, BOTH, self.route(mask))

    def places(self, me):
        mine = sum(((me & mask) != 0).astype(i32) << step for step, mask in enumerate(self.lead))
        return jnp.arange(1 << len(self.lead), dtype=i32) ^ mine


def together(*values):
    return lax.optimization_barrier(values)


def shards(
    plan,
    entity_rows,
    entity_state,
    relation_rows,
    relation_state,
    conv_weight,
    conv_bias,
    fc_weight,
    fc_bias,
    head_ids,
    rel_ids,
    tail_ids,
    neg_ids,
):
    number = head_ids.shape[1]
    negatives = neg_ids.shape[1]
    count = relation_rows.shape[0]
    wide = count + -count % LANES
    features = fc_weight.shape[0]
    group = 1 << len(plan.lead)
    send = plan.send
    me = lax.axis_index("group") * plan.shards + lax.axis_index("shard")
    place = plan.places(me)
    ent = entity_rows.T
    ent_state = entity_state[None, :]
    rel = relation_rows.T
    rel_state = relation_state[None, :]
    bias2 = fc_bias[None, :]
    next_door, beyond = plan.near[-1], plan.near[:-1]

    def asked_rows(answer, bit):
        near = send(answer, plan.partner(bit))
        side = send(answer[number:], plan.partner(bit) | next_door)
        return near, side

    wanted = call(
        wanted_kernel,
        "wanted",
        1,
        [shaped((2, LANES), i32)] * ROUNDS,
        (tail_ids, neg_ids),
        [pltpu.VMEM(tail_ids.shape, i32), pltpu.VMEM(neg_ids.shape, i32), pltpu.SemaphoreType.DMA((2,))],
        far=(0, 1),
    )
    requested = [send(wanted[0], plan.partner(0))]
    rel_first, rel_later, state_later = call(
        rows_kernel,
        "relation_rows",
        1,
        [shaped((D, number)), shaped((D, number)), shaped((1, number))],
        (rel_ids, rel, rel_state),
        [pltpu.VMEM((D, wide), f32)],
    )
    requested[0], rel_first, rel_later, state_later = together(
        requested[0], rel_first, rel_later, state_later
    )
    answer_shape = shaped((number + negatives, D), bf16)
    (answer,) = call(
        functools.partial(answer_kernel, negatives), "answer", 1, [answer_shape], (requested[0], ent)
    )
    near, side = asked_rows(answer, 0)
    taps = jnp.tile(conv_weight.reshape(FILTERS, 9).T.astype(f32), (1, WIDE // FILTERS))
    bias = jnp.tile(conv_bias[None, :], (1, WIDE // FILTERS))
    pre2, slopes, fc, band, band_t = call(
        first_kernel,
        "first_forward",
        6,
        [
            shaped((number, D)),
            shaped((PAIRS, number, WIDE)),
            shaped((PAIRS, WIDE, D), bf16),
            shaped((WINDOW, WIDE), bf16),
            shaped((WIDE, LANES), bf16),
        ],
        (fc_weight.T, taps, head_ids, ent, rel_first, bias, bias2),
        [
            pltpu.VMEM((PIXELS, number), f32),
            pltpu.VMEM((PAIRS, number, WIDE), bf16),
            pltpu.VMEM((features, LANES), f32),
            pltpu.VMEM((features, LANES), f32),
            pltpu.VMEM((D, features), bf16),
            pltpu.SemaphoreType.DMA((PAIRS,)),
        ],
        limit=LIMP,
        far=(0,),
        near_out=(1, 2),
    )
    near, side, band = together(near, side, band)
    negset = jnp.concatenate([near[number:], side], axis=0)
    for mask in beyond:
        negset = jnp.concatenate([negset, send(negset, mask)], axis=0)
    requested.append(send(wanted[1], plan.partner(1)))
    near, negset = together(near, negset)
    rel_others = send(rel_ids, 1)
    negset = jnp.concatenate([negset, send(negset, 1)], axis=0)

    def lay(sources):
        return [pltpu.VMEM((PACK, sources * LANES), bf16), pltpu.VMEM((8, sources * LANES), i32)]

    sums = []
    for r in range(ROUNDS):
        last = r == ROUNDS - 1
        if r > 0:
            pre2, slopes, fc, ent = call(
                functools.partial(forward_kernel, r),
                "forward",
                2.5,
                [
                    shaped((number, D)),
                    shaped((PAIRS, number, WIDE)),
                    shaped(fc.shape, bf16),
                    shaped(ent.shape),
                ],
                (fc, head_ids, ent, *rel_inputs, band, bias, bias2),
                [pltpu.VMEM((PIXELS, number), f32), pltpu.VMEM((PAIRS, number, WIDE), bf16)],
                limit=LIM,
                near=(0, 2),
                near_out=(1, 2, 3),
                alias={0: 2, 2: 3},
            )
        grad2, tail_grad, neg_part = call(
            score_kernel,
            "scores",
            1,
            [shaped((number, D), bf16), shaped((number, D)), shaped((negset.shape[0], D))],
            (pre2, near[:number], negset),
        )
        if r == 0:
            grad2, neg_part, rel_others = together(grad2, neg_part, rel_others)
        half = neg_part.shape[0] // 2
        arrived = send(neg_part[half:], 1)
        pack, head_grad, fc = call(
            functools.partial(backward_kernel, r),
            "backward",
            3,
            [shaped((PACK, number), bf16), shaped((D, number)), shaped(fc.shape, bf16)],
            (fc, rel_ids, grad2, slopes, band_t),
            [
                pltpu.VMEM((PAIRS, number, WIDE), bf16),
                pltpu.VMEM((PIXELS, number), f32),
            ],
            limit=LIM,
            near=(0, 3),
            near_out=(2,),
            alias={0: 2},
        )
        pack, arrived = together(pack, arrived)
        share = neg_part[:half] + arrived
        packs = pack[None]
        lead = list(plan.lead)
        if last:
            before = call(
                functools.partial(sums_kernel, (3, 0)),
                "early_sums",
                3,
                [shaped((D, wide))] * 2,
                (place, *groups[:3]),
                lay(3 * group),
                scalars=1,
            )
        back = list(reversed(beyond))
        for step, mask in enumerate(lead):
            came = send(packs, mask)
            if step < len(back):
                half = share.shape[0] // 2
                arrived = send(share[half:], back[step])
                if last:
                    came, arrived, *before = together(came, arrived, *before)
                    (part,) = call(
                        functools.partial(sums_kernel, (1, 2)),
                        "late_sums",
                        1,
                        [shaped((D, wide))],
                        (place, groups[3], *before),
                        lay(group),
                        scalars=1,
                    )
                else:
                    came, arrived, requested[1] = together(came, arrived, requested[1])
                share = share[:half] + arrived
            elif step == len(lead) - 1:
                own_back = jnp.concatenate([tail_grad, share[:negatives]], axis=0).astype(bf16)
                side_back = share[negatives:].astype(bf16)
                to_owner = send(own_back, plan.partner(r))
                to_side = send(side_back, plan.partner(r) | next_door)
                if last:
                    came, part = together(came, part)
            packs = jnp.concatenate([packs, came], axis=0)
        one, other = plan.far[-2:]
        across = send(packs, one)
        along = send(packs, other)
        if last:
            across, along, to_owner, to_side = together(across, along, to_owner, to_side)
        out_shape = [shaped(ent.shape), shaped(ent_state.shape)]
        outs = call(
            functools.partial(entity_kernel, r, negatives),
            "entity_update",
            1.5,
            out_shape if last else out_shape + [answer_shape],
            (
                head_ids,
                requested[r],
                requested[min(r + 1, ROUNDS - 1)],
                ent,
                ent_state,
                head_grad,
                to_owner,
                to_side,
            ),
            near=(3,) if last else (),
            near_out=() if last else (0,),
        )
        ent, ent_state = outs[:2]
        if last:
            across, along, part = together(across, along, part)
            corner = send(across, other)
            early = call(
                functools.partial(sums_kernel, (3, 0)),
                "early_sums",
                3,
                [shaped((D, wide))] * 2,
                (place, packs, across, along),
                lay(3 * group),
                scalars=1,
            )
            corner, part, ent, ent_state, *early = together(corner, part, ent, ent_state, *early)
            sums = [part, send(part, 1)]
            (part,) = call(
                functools.partial(sums_kernel, (1, 2)),
                "late_sums",
                1,
                [shaped((D, wide))],
                (place, corner, *early),
                lay(group),
                scalars=1,
            )
            sums += [part, send(part, 1)]
        else:
            near, side = asked_rows(outs[2], r + 1)
            corner = send(across, other)
            groups = (packs, across, along, corner)
            near, side = together(near, side)
            negset = jnp.concatenate([near[number:], side], axis=0)
            for mask in beyond:
                negset = jnp.concatenate([negset, send(negset, mask)], axis=0)
            own, partial = call(
                functools.partial(need_kernel, r + 1),
                "need",
                1.5,
                [shaped((PACK, number))] * 2,
                (place, *groups, rel_ids, rel_others),
                lay(4 * group),
                scalars=1,
            )
            negset, own, partial = together(negset, own, partial)
            rel_inputs = (own, send(partial, 1), rel_later, state_later)
            negset = jnp.concatenate([negset, send(negset, 1)], axis=0)
    rel, rel_state = call(
        relation_kernel, "relation_update", 2, [shaped((D, count)), shaped((count,))], (rel, rel_state, *sums)
    )
    return (ent.T, ent_state.reshape(-1), rel.T, rel_state)


def solution(mesh):
    plan = Plan(mesh.shape["group"], mesh.shape["shard"])
    in_specs = (
        P(BOTH, None),
        P(BOTH),
        P(),
        P(),
        P(),
        P(),
        P(),
        P(),
        P(None, BOTH),
        P(None, BOTH),
        P(None, BOTH),
        P(None, BOTH),
    )
    out_specs = (P(BOTH, None), P(BOTH), P(), P())
    return jax.shard_map(
        functools.partial(shards, plan),
        mesh=mesh,
        in_specs=in_specs,
        out_specs=out_specs,
        check_vma=False,
    )
```

```python
import functools

import jax
import jax.numpy as jnp
from jax import lax
from jax.experimental import pallas as pl
from jax.experimental.pallas import tpu as pltpu
from jax.sharding import PartitionSpec as P

EMB_W = 20
D = 200
FILTERS = 32
PIXELS = 400
SIDE = 18
PAIRS = 9
WINDOW = 80
WIDE = 1152
PACK = 208
LANES = 128
ROUNDS = 2
LIM = 24
LIMP = 28

negative_weight = 0.03125
learn_rate = 0.5

f32 = jnp.float32
bf16 = jnp.bfloat16
i32 = jnp.int32
BOTH = ("group", "shard")
VMEM = pl.BlockSpec(memory_space=pltpu.VMEM)
SMEM = pl.BlockSpec(memory_space=pltpu.SMEM)
HBM = pl.BlockSpec(memory_space=pltpu.HBM)


def shaped(shape, dtype=f32):
    return jax.ShapeDtypeStruct(shape, dtype)


def call(kernel, name, micros, out_shape, args, scratch=(), scalars=0, limit=16, far=(), near=(), near_out=(), alias=None):
    places = [SMEM] * scalars + [VMEM] * (len(args) - scalars)
    args = [
        pltpu.with_memory_space_constraint(arg, pltpu.HBM)
        if index in far
        else pltpu.with_memory_space_constraint(arg, pltpu.VMEM)
        if index in near
        else arg
        for index, arg in enumerate(args)
    ]
    return pl.pallas_call(
        kernel,
        out_shape=[
            pltpu.VMEM(out.shape, out.dtype) if index in near_out else out
            for index, out in enumerate(out_shape)
        ],
        input_output_aliases=alias or {},
        in_specs=[HBM if index in far else spec for index, spec in enumerate(places)],
        out_specs=[VMEM] * len(out_shape),
        scratch_shapes=list(scratch),
        compiler_params=pltpu.CompilerParams(vmem_limit_bytes=limit * 1024 * 1024),
        cost_estimate=pl.CostEstimate(
            flops=int(micros * 3e9), bytes_accessed=int(micros * 9e6), transcendentals=0
        ),
        name=name,
    )(*args)


def sigmoid(values):
    return 0.5 * jnp.tanh(0.5 * values) + 0.5


def dot(left, right):
    return jnp.dot(left, right, preferred_element_type=f32)


def dot_nt(left, right):
    return lax.dot_general(left, right, (((1,), (1,)), ((), ())), preferred_element_type=f32)


def dot_tn(left, right):
    return lax.dot_general(left, right, (((0,), (0,)), ((), ())), preferred_element_type=f32)


def as_column(row):
    return jnp.transpose(jnp.broadcast_to(row.astype(f32), (LANES, LANES)))


def hits(names_row, count, first=0):
    spot = lax.broadcasted_iota(i32, (count, names_row.shape[1]), 0) + first
    return jnp.where(spot == names_row, 1.0, 0.0).astype(bf16)


def halves(values):
    high = values.astype(bf16)
    return high, (values - high.astype(f32)).astype(bf16)


def padded(values, lanes):
    rest = lanes - values.shape[1]
    return jnp.concatenate([values, jnp.zeros((values.shape[0], rest), values.dtype)], axis=1)


def turned(values):
    rest = -values.shape[0] % LANES
    return jnp.transpose(jnp.concatenate([values, jnp.zeros((rest, D), f32)], axis=0))


def wanted_kernel(tails_hbm, negatives_hbm, *refs):
    outs, (tails_ref, negatives_ref, sems) = refs[:ROUNDS], refs[ROUNDS:]
    copies = [
        pltpu.make_async_copy(tails_hbm, tails_ref, sems.at[0]),
        pltpu.make_async_copy(negatives_hbm, negatives_ref, sems.at[1]),
    ]
    for copy in copies:
        copy.start()
    for copy in copies:
        copy.wait()
    for index, out in enumerate(outs):
        out[0:1, :] = tails_ref[index : index + 1, :]
        out[1:2, :] = padded(negatives_ref[index : index + 1, :], LANES)


def pick_answer(table, ids_ref, negatives, out):
    count = table.shape[1]
    number = out.shape[0] - negatives
    tails = dot(table, hits(ids_ref[0:1, :], count))
    out[:number, :] = jnp.transpose(tails).astype(bf16)
    negs = dot(table, hits(ids_ref[1:2, :], count))
    out[number:, :] = jnp.transpose(negs)[:negatives, :].astype(bf16)


def answer_kernel(negatives, ids_ref, ent_ref, out):
    pick_answer(ent_ref[...].astype(bf16), ids_ref, negatives, out)


def prepare(fc_hbm, taps_ref, band_out, band_t_out, fc_ref, sems, left, right):
    copies = []
    for pair in range(PAIRS):
        at = pl.ds(pair * WIDE, WIDE)
        copies.append(pltpu.make_async_copy(fc_hbm.at[:, at], fc_ref.at[:, at], sems.at[pair]))
        copies[-1].start()
    group = lax.broadcasted_iota(i32, (WINDOW, WIDE), 1) >> 5
    start = group + jnp.where(group >= SIDE, EMB_W - SIDE, 0)
    gap = lax.broadcasted_iota(i32, (WINDOW, WIDE), 0) - start
    band = jnp.zeros((WINDOW, WIDE), f32)
    for row_off in range(3):
        for col_off in range(3):
            tap = row_off * 3 + col_off
            hit = gap == EMB_W * row_off + col_off
            band = jnp.where(hit, taps_ref[tap : tap + 1, :], band)
    band_out[...] = band.astype(bf16)
    band_t_out[...] = jnp.transpose(
        jnp.concatenate([band, jnp.zeros((LANES - WINDOW, WIDE), f32)], axis=0)
    ).astype(bf16)
    for copy in copies:
        copy.wait()
    blank = jnp.zeros((2 * LANES - D, LANES), f32)
    for index in range(fc_ref.shape[1] // LANES):
        at = slice(index * LANES, (index + 1) * LANES)
        block = fc_ref[:, at].astype(f32)
        left[at, :] = jnp.transpose(block[:LANES])
        right[at, :] = jnp.transpose(jnp.concatenate([block[LANES:], blank], axis=0))


def regroup(pair, fc_out, left, right):
    spots = SIDE * SIDE
    each = spots // PAIRS
    for index in range(each):
        low = left[pl.ds(pair * each + index, FILTERS, stride=spots), :]
        high = right[pl.ds(pair * each + index, FILTERS, stride=spots), :]
        at = slice(index * FILTERS, (index + 1) * FILTERS)
        fc_out[pair, at, :LANES] = low.astype(bf16)
        fc_out[pair, at, LANES:] = high[:, : D - LANES].astype(bf16)


def rows_kernel(ids_ref, rel_ref, state_ref, first_out, later_out, state_out, table):
    count = rel_ref.shape[1]
    whole = count // LANES * LANES
    table[:, :whole] = rel_ref[:, :whole]
    rest = jnp.concatenate(
        [rel_ref[:, whole:], jnp.zeros((D, LANES - count + whole), f32)], axis=1
    )
    table[:, whole:] = rest
    values = table[...]
    wide = values.shape[1]
    high = values.astype(bf16)
    first_out[...] = dot(high, hits(ids_ref[0:1, :], wide))
    left = values - high.astype(f32)
    middle = left.astype(bf16)
    low = (left - middle.astype(f32)).astype(bf16)
    hit = hits(ids_ref[1:2, :], wide)
    later_out[...] = dot(high, hit) + dot(middle, hit) + dot(low, hit)
    sums = padded(state_ref[...], wide)
    names = ids_ref[1:2, :]
    total = jnp.zeros((LANES, LANES), f32)
    for block in range(wide // LANES):
        states = as_column(sums[:, block * LANES : (block + 1) * LANES])
        spot = lax.broadcasted_iota(i32, (LANES, LANES), 0) + block * LANES
        total = total + jnp.where(spot == names, states, 0.0)
    state_out[...] = jnp.sum(total, axis=0, keepdims=True)


def convolve(heads, rel_rows, ent_ref, band_ref, bias_ref, fcb_ref, fc_ref, pre2_out, slopes, picture, work, ready):
    table = ent_ref[...].astype(bf16)
    picture[:D, :] = dot(table, hits(heads, table.shape[1]))
    picture[D:, :] = rel_rows
    pre2 = jnp.zeros(pre2_out.shape, f32)
    for pair in range(PAIRS):
        first = pair * 2 * EMB_W
        window = jnp.transpose(picture[first : first + WINDOW, :]).astype(bf16)
        pre1 = dot(window, band_ref[...]) + bias_ref[...]
        sigma = sigmoid(pre1)
        act = pre1 * sigma
        slopes[pair] = sigma + act * (1.0 - sigma)
        work[pair] = act.astype(bf16)
        ready(pair)
        pre2 = pre2 + dot(work[pair], fc_ref[pair])
    pre2_out[...] = pre2 + fcb_ref[...]


def first_kernel(
    fc_hbm, taps_ref, heads_ref, ent_ref, rel_ref, bias_ref, fcb_ref,
    pre2_out, slopes, fc_out, band_out, band_t_out,
    picture, work, left, right, fc_ref, sems,
):
    prepare(fc_hbm, taps_ref, band_out, band_t_out, fc_ref, sems, left, right)

    def ready(pair):
        regroup(pair, fc_out, left, right)

    convolve(
        heads_ref[0:1, :], rel_ref[...], ent_ref, band_out, bias_ref, fcb_ref, fc_out,
        pre2_out, slopes, picture, work, ready,
    )


def forward_kernel(
    round_index, fc_ref, heads_ref, ent_ref, own_ref, other_ref, rows_ref, state_ref, band_ref, bias_ref, fcb_ref,
    pre2_out, slopes, fc_same, ent_same, picture, work,
):
    gradient = (own_ref[...] + other_ref[...])[:D, :]
    state = state_ref[...] + jnp.mean(gradient * gradient, axis=0, keepdims=True)
    rel_rows = rows_ref[...] - gradient * (learn_rate * lax.rsqrt(state))
    rel_rows = rel_rows.astype(bf16).astype(f32)
    convolve(
        heads_ref[round_index : round_index + 1, :], rel_rows, ent_ref, band_ref, bias_ref, fcb_ref, fc_ref,
        pre2_out, slopes, picture, work, lambda pair: None,
    )


def score_kernel(pre2_ref, tail_ref, neg_ref, grad_out, tail_out, neg_out):
    pre2 = pre2_ref[...]
    sigma = sigmoid(pre2)
    value = pre2 * sigma
    slope = sigma + value * (1.0 - sigma)
    query = value.astype(bf16)
    query32 = query.astype(f32)
    tails = tail_ref[...].astype(f32)
    pos_grad = -sigmoid(-jnp.sum(query32 * tails, axis=1, keepdims=True))
    negset = neg_ref[...]
    neg_grad = (negative_weight * sigmoid(dot_nt(query, negset))).astype(bf16)
    query_grad = pos_grad * tails + dot(neg_grad, negset)
    grad_out[...] = (query_grad * slope).astype(bf16)
    tail_out[...] = pos_grad * query32
    neg_out[...] = dot_tn(neg_grad, query)


def backward_kernel(
    round_index, fc_ref, relations_ref, grad_ref, slopes, band_t_ref, pack_out, head_out, _, work, total
):
    pre2_grad = grad_ref[...]
    total[...] = jnp.zeros_like(total)
    for pair in range(PAIRS):
        act_grad = dot_nt(pre2_grad, fc_ref[pair])
        work[pair] = (act_grad * slopes[pair]).astype(bf16)
        part = dot(work[pair], band_t_ref[...])
        at = slice(pair * 2 * EMB_W, pair * 2 * EMB_W + WINDOW)
        total[at, :] = total[at, :] + jnp.transpose(part)[:WINDOW, :]
    head_out[...] = total[:D, :]
    relations = relations_ref[round_index : round_index + 1, :]
    high = relations >> 6
    low = relations - (high << 6)
    spare = lax.broadcasted_iota(i32, (PACK - D, LANES), 0)
    codes = jnp.where(spare == 0, high, jnp.where(spare == 1, low, 0)).astype(f32)
    pack_out[...] = jnp.concatenate([total[D:, :], codes], axis=0).astype(bf16)


def entity_kernel(
    round_index, negatives, heads_ref, asked_ref, next_ref, ent_ref, state_ref, head_ref, back_ref, other_ref, *outs
):
    count = ent_ref.shape[1]
    number = back_ref.shape[0] - negatives
    back = back_ref[...].astype(f32)
    back = jnp.concatenate([back[:number, :], back[number:, :] + other_ref[...].astype(f32)], axis=0)
    grads = jnp.concatenate([head_ref[...], turned(back)], axis=1)
    high, low = halves(grads)
    named = jnp.concatenate(
        [heads_ref[round_index : round_index + 1, :], asked_ref[0:1, :], asked_ref[1:2, :]], axis=1
    )
    both = dot_nt(jnp.concatenate([high, low], axis=0), hits(named, count))
    gradient = both[:D, :] + both[D:, :]
    state = state_ref[...] + jnp.mean(gradient * gradient, axis=0, keepdims=True)
    rows = ent_ref[...] - gradient * (learn_rate * lax.rsqrt(state))
    outs[0][...] = rows
    outs[1][...] = state
    if len(outs) > 2:
        pick_answer(rows.astype(bf16), next_ref, negatives, outs[2])


def lay_packs(place_ref, groups, grads, names):
    index = 0
    for group in groups:
        for inner in range(group.shape[0]):
            at = slice(index * LANES, (index + 1) * LANES)
            block = group[place_ref[inner]]
            grads[:, at] = block
            codes = block[PACK - 16 :, :].astype(f32)[D - PACK + 16 :, :]
            names[0:1, at] = (codes[0:1, :] * 64.0 + codes[1:2, :]).astype(i32)
            index += 1


def need_kernel(round_index, place_ref, *refs):
    groups, (ids_ref, others_ref, own_out, send_out, grads, names) = refs[:4], refs[4:]
    lay_packs(place_ref, groups, grads, names)
    wide = names.shape[1]
    for ids, out in ((others_ref, send_out), (ids_ref, own_out)):
        column = as_column(ids[round_index : round_index + 1, :])
        hit = jnp.concatenate(
            [
                jnp.where(
                    column == names[0:1, at : at + LANES].astype(f32), 1.0, 0.0
                ).astype(bf16)
                for at in range(0, wide, LANES)
            ],
            axis=1,
        )
        out[...] = jnp.transpose(dot_nt(hit, grads[...]))


def sums_kernel(kinds, place_ref, *refs):
    packs, before, refs = refs[: kinds[0]], refs[kinds[0] : sum(kinds)], refs[sum(kinds) :]
    outs, grads, names = refs[:-2], refs[-2], refs[-1]
    lay_packs(place_ref, packs, grads, names)
    size = names.shape[1] // len(packs)
    for first in range(0, outs[0].shape[1], LANES):
        at = slice(first, first + LANES)
        hit = hits(names[0:1, :], LANES, first)
        parts = [
            dot_nt(grads[:, k * size : (k + 1) * size], hit[:, k * size : (k + 1) * size])[:D, :]
            for k in range(len(packs))
        ]
        if len(packs) == 4:
            outs[0][:, at] = (parts[0] + parts[1]) + (parts[2] + parts[3])
        elif len(packs) == 3:
            outs[0][:, at] = parts[0] + parts[1]
            outs[1][:, at] = parts[2]
        else:
            outs[0][:, at] = before[0][:, at] + (before[1][:, at] + parts[0])


def relation_kernel(rel_ref, state_ref, *refs):
    rows = rel_ref[...]
    state = state_ref[...]
    count = rows.shape[1]
    for index in range(ROUNDS):
        gradient = refs[2 * index][:, :count] + refs[2 * index + 1][:, :count]
        state = state + jnp.mean(gradient * gradient, axis=0, keepdims=True)
        rows = rows - gradient * (learn_rate * lax.rsqrt(state))
    refs[2 * ROUNDS][...] = rows
    refs[2 * ROUNDS + 1][...] = state[0]


class Plan:
    def __init__(self, groups, shards):
        self.total = groups * shards
        self.shards = shards
        self.near = [1 << bit for bit in range(1, shards.bit_length() - 1)]
        self.far = [shards << bit for bit in range(groups.bit_length() - 1)]
        self.lead = self.near[::-1] + self.far[:-2]

    def route(self, mask):
        return [(at, at ^ mask) for at in range(self.total)]

    def partner(self, bit):
        return self.shards << bit

    def send(self, block, mask):
        return lax.ppermute(block, BOTH, self.route(mask))

    def places(self, me):
        mine = sum(((me & mask) != 0).astype(i32) << step for step, mask in enumerate(self.lead))
        return jnp.arange(1 << len(self.lead), dtype=i32) ^ mine


def together(*values):
    return lax.optimization_barrier(values)


def shards(
    plan,
    entity_rows,
    entity_state,
    relation_rows,
    relation_state,
    conv_weight,
    conv_bias,
    fc_weight,
    fc_bias,
    head_ids,
    rel_ids,
    tail_ids,
    neg_ids,
):
    number = head_ids.shape[1]
    negatives = neg_ids.shape[1]
    count = relation_rows.shape[0]
    wide = count + -count % LANES
    features = fc_weight.shape[0]
    group = 1 << len(plan.lead)
    send = plan.send
    me = lax.axis_index("group") * plan.shards + lax.axis_index("shard")
    place = plan.places(me)
    ent = entity_rows.T
    ent_state = entity_state[None, :]
    rel = relation_rows.T
    rel_state = relation_state[None, :]
    bias2 = fc_bias[None, :]
    next_door, beyond = plan.near[-1], plan.near[:-1]

    def asked_rows(answer, bit):
        near = send(answer, plan.partner(bit))
        side = send(answer[number:], plan.partner(bit) | next_door)
        return near, side

    wanted = call(
        wanted_kernel,
        "wanted",
        1,
        [shaped((2, LANES), i32)] * ROUNDS,
        (tail_ids, neg_ids),
        [pltpu.VMEM(tail_ids.shape, i32), pltpu.VMEM(neg_ids.shape, i32), pltpu.SemaphoreType.DMA((2,))],
        far=(0, 1),
    )
    requested = [send(wanted[0], plan.partner(0))]
    rel_first, rel_later, state_later = call(
        rows_kernel,
        "relation_rows",
        1,
        [shaped((D, number)), shaped((D, number)), shaped((1, number))],
        (rel_ids, rel, rel_state),
        [pltpu.VMEM((D, wide), f32)],
    )
    requested[0], rel_first, rel_later, state_later = together(
        requested[0], rel_first, rel_later, state_later
    )
    answer_shape = shaped((number + negatives, D), bf16)
    (answer,) = call(
        functools.partial(answer_kernel, negatives), "answer", 1, [answer_shape], (requested[0], ent)
    )
    near, side = asked_rows(answer, 0)
    taps = jnp.tile(conv_weight.reshape(FILTERS, 9).T.astype(f32), (1, WIDE // FILTERS))
    bias = jnp.tile(conv_bias[None, :], (1, WIDE // FILTERS))
    pre2, slopes, fc, band, band_t = call(
        first_kernel,
        "first_forward",
        6,
        [
            shaped((number, D)),
            shaped((PAIRS, number, WIDE)),
            shaped((PAIRS, WIDE, D), bf16),
            shaped((WINDOW, WIDE), bf16),
            shaped((WIDE, LANES), bf16),
        ],
        (fc_weight.T, taps, head_ids, ent, rel_first, bias, bias2),
        [
            pltpu.VMEM((PIXELS, number), f32),
            pltpu.VMEM((PAIRS, number, WIDE), bf16),
            pltpu.VMEM((features, LANES), f32),
            pltpu.VMEM((features, LANES), f32),
            pltpu.VMEM((D, features), bf16),
            pltpu.SemaphoreType.DMA((PAIRS,)),
        ],
        limit=LIMP,
        far=(0,),
        near_out=(1, 2),
    )
    near, side, band = together(near, side, band)
    negset = jnp.concatenate([near[number:], side], axis=0)
    for mask in beyond:
        negset = jnp.concatenate([negset, send(negset, mask)], axis=0)
    requested.append(send(wanted[1], plan.partner(1)))
    near, negset = together(near, negset)
    rel_others = send(rel_ids, 1)
    negset = jnp.concatenate([negset, send(negset, 1)], axis=0)

    def lay(sources):
        return [pltpu.VMEM((PACK, sources * LANES), bf16), pltpu.VMEM((8, sources * LANES), i32)]

    sums = []
    for r in range(ROUNDS):
        last = r == ROUNDS - 1
        if r > 0:
            pre2, slopes, fc, ent = call(
                functools.partial(forward_kernel, r),
                "forward",
                2.5,
                [
                    shaped((number, D)),
                    shaped((PAIRS, number, WIDE)),
                    shaped(fc.shape, bf16),
                    shaped(ent.shape),
                ],
                (fc, head_ids, ent, *rel_inputs, band, bias, bias2),
                [pltpu.VMEM((PIXELS, number), f32), pltpu.VMEM((PAIRS, number, WIDE), bf16)],
                limit=LIM,
                near=(0, 2),
                near_out=(1, 2, 3),
                alias={0: 2, 2: 3},
            )
        grad2, tail_grad, neg_part = call(
            score_kernel,
            "scores",
            1,
            [shaped((number, D), bf16), shaped((number, D)), shaped((negset.shape[0], D))],
            (pre2, near[:number], negset),
        )
        if r == 0:
            grad2, neg_part, rel_others = together(grad2, neg_part, rel_others)
        half = neg_part.shape[0] // 2
        arrived = send(neg_part[half:], 1)
        pack, head_grad, fc = call(
            functools.partial(backward_kernel, r),
            "backward",
            3,
            [shaped((PACK, number), bf16), shaped((D, number)), shaped(fc.shape, bf16)],
            (fc, rel_ids, grad2, slopes, band_t),
            [
                pltpu.VMEM((PAIRS, number, WIDE), bf16),
                pltpu.VMEM((PIXELS, number), f32),
            ],
            limit=LIM,
            near=(0, 3),
            near_out=(2,),
            alias={0: 2},
        )
        pack, arrived = together(pack, arrived)
        share = neg_part[:half] + arrived
        packs = pack[None]
        lead = list(plan.lead)
        if last:
            before = call(
                functools.partial(sums_kernel, (3, 0)),
                "early_sums",
                3,
                [shaped((D, wide))] * 2,
                (place, *groups[:3]),
                lay(3 * group),
                scalars=1,
            )
        back = list(reversed(beyond))
        for step, mask in enumerate(lead):
            came = send(packs, mask)
            if step < len(back):
                half = share.shape[0] // 2
                arrived = send(share[half:], back[step])
                if last:
                    came, arrived, *before = together(came, arrived, *before)
                    (part,) = call(
                        functools.partial(sums_kernel, (1, 2)),
                        "late_sums",
                        1,
                        [shaped((D, wide))],
                        (place, groups[3], *before),
                        lay(group),
                        scalars=1,
                    )
                else:
                    came, arrived, requested[1] = together(came, arrived, requested[1])
                share = share[:half] + arrived
            elif step == len(lead) - 1:
                own_back = jnp.concatenate([tail_grad, share[:negatives]], axis=0).astype(bf16)
                side_back = share[negatives:].astype(bf16)
                to_owner = send(own_back, plan.partner(r))
                to_side = send(side_back, plan.partner(r) | next_door)
                if last:
                    came, part = together(came, part)
            packs = jnp.concatenate([packs, came], axis=0)
        one, other = plan.far[-2:]
        across = send(packs, one)
        along = send(packs, other)
        out_shape = [shaped(ent.shape), shaped(ent_state.shape)]
        outs = call(
            functools.partial(entity_kernel, r, negatives),
            "entity_update",
            1.5,
            out_shape if last else out_shape + [answer_shape],
            (
                head_ids,
                requested[r],
                requested[min(r + 1, ROUNDS - 1)],
                ent,
                ent_state,
                head_grad,
                to_owner,
                to_side,
            ),
            near=(3,) if last else (),
            near_out=() if last else (0,),
        )
        ent, ent_state = outs[:2]
        if last:
            across, along, part = together(across, along, part)
            corner = send(across, other)
            early = call(
                functools.partial(sums_kernel, (3, 0)),
                "early_sums",
                3,
                [shaped((D, wide))] * 2,
                (place, packs, across, along),
                lay(3 * group),
                scalars=1,
            )
            corner, part, ent, ent_state, *early = together(corner, part, ent, ent_state, *early)
            sums = [part, send(part, 1)]
            (part,) = call(
                functools.partial(sums_kernel, (1, 2)),
                "late_sums",
                1,
                [shaped((D, wide))],
                (place, corner, *early),
                lay(group),
                scalars=1,
            )
            sums += [part, send(part, 1)]
        else:
            near, side = asked_rows(outs[2], r + 1)
            corner = send(across, other)
            groups = (packs, across, along, corner)
            near, side = together(near, side)
            negset = jnp.concatenate([near[number:], side], axis=0)
            for mask in beyond:
                negset = jnp.concatenate([negset, send(negset, mask)], axis=0)
            own, partial = call(
                functools.partial(need_kernel, r + 1),
                "need",
                1.5,
                [shaped((PACK, number))] * 2,
                (place, *groups, rel_ids, rel_others),
                lay(4 * group),
                scalars=1,
            )
            negset, own, partial = together(negset, own, partial)
            rel_inputs = (own, send(partial, 1), rel_later, state_later)
            negset = jnp.concatenate([negset, send(negset, 1)], axis=0)
    rel, rel_state = call(
        relation_kernel, "relation_update", 2, [shaped((D, count)), shaped((count,))], (rel, rel_state, *sums)
    )
    return (ent.T, ent_state.reshape(-1), rel.T, rel_state)


def solution(mesh):
    plan = Plan(mesh.shape["group"], mesh.shape["shard"])
    in_specs = (
        P(BOTH, None),
        P(BOTH),
        P(),
        P(),
        P(),
        P(),
        P(),
        P(),
        P(None, BOTH),
        P(None, BOTH),
        P(None, BOTH),
        P(None, BOTH),
    )
    out_specs = (P(BOTH, None), P(BOTH), P(), P())
    return jax.shard_map(
        functools.partial(shards, plan),
        mesh=mesh,
        in_specs=in_specs,
        out_specs=out_specs,
        check_vma=False,
    )
```
